512 devices in a mesh: ep: 128 (over y_hi, z, x), rep: 4 (over y_lo, core).
Axes of the slice: x: 4, y: 4 (y_hi: 2, y_lo: 2; y = y_hi * 2 + y_lo), z: 16, core: 2. Of those that a mesh axis runs over, the one named last changes fastest.
Arguments:
- out_grad: bfloat16 [4096, 3584], P('ep', 'rep'), may hold values from -0.3984375 to 0.3984375
- route_weight: float32 [4096, 4], P('ep'), may hold values from 0.05 to 0.5
- expert_ids: int32 [4096, 4], P('ep'), may hold values from 0 to 95, all different within a row; in each aligned block of 32 rows (0 to 31, 32 to 63, ...) at most 2 rows name the same one
- slot_expert: int32 [128], replicated, may hold values from 0 to 95, as said below
- replica_pick: int32 [128, 96], P('ep'), may hold values from 0 to 1, as said below
- saved_gu: bfloat16 [128, 256, 2, 1024], P('ep', None, None, 'rep'), may hold values from -6 to 6
- down_weight: bfloat16 [128, 1024, 3584], P('ep', None, 'rep'), as said below
Outputs:
- down_grad: bfloat16 [128, 1024, 3584], P('ep', None, 'rep')
- route_grad: float32 [4096, 4], P('ep')
The draws below stay inside these ranges and needn't reach their ends.
Inputs may be any that keep to these rules, and one draw needn't show every extreme that they name: `expert_ids`: no expert is named by more than 2 of the tokens of one index of ep. `slot_expert`: every expert is held by one or two slots; an expert held by two slots is held by slots s and s + 64. `replica_pick`: entry [i, e] is less than the number of slots that hold expert e. `down_weight`: slots that hold the same expert hold equal weights.
All inputs are finite; a program needn't handle non-finite values.
Results may differ from the reference program's by a relative error of at most 0.0067.
Values may be sent and summed in bfloat16 or wider, within the bound.
No kernel may reach another device: no remote copies, remote signals or barrier semaphores. Data moves between devices by JAX's collectives and lax.ppermute only.
A program may use at most 64 MiB of HBM per device.

```python
import math
import jax
import jax.numpy as jnp
import numpy as np
from jax import lax

D = 3584
F = 1024
TOPK = 4
TOK_DEV = 32
TOKENS = 4096
SLOTS = 128
EXPERTS = 96
PAIR = 2
ROWS_SLOT = 256
N_EP = 128


def slot_plan(key):
    half = SLOTS // 2
    hot_count = SLOTS - EXPERTS
    first, second = jax.random.split(key, 2)
    pair_order = jax.random.permutation(first, half).astype(jnp.int32)
    expert_order = jax.random.permutation(second, EXPERTS).astype(jnp.int32)
    place = jnp.arange(half, dtype=jnp.int32)
    is_hot = place < hot_count
    lower_pos = jnp.where(is_hot, place, hot_count + 2 * (place - hot_count))
    upper_pos = jnp.where(is_hot, place, hot_count + 2 * (place - hot_count) + 1)
    lower_pos = jnp.clip(lower_pos, 0, EXPERTS - 1)
    upper_pos = jnp.clip(upper_pos, 0, EXPERTS - 1)
    lower_ids = expert_order[lower_pos]
    upper_ids = expert_order[upper_pos]
    plan = jnp.zeros((SLOTS,), jnp.int32).at[pair_order].set(lower_ids).at[pair_order + half].set(upper_ids)
    return plan.astype(jnp.int32)


def draw_slot_expert(key, part):
    return slot_plan(key)


def draw_replica_pick(key, part):
    plan = slot_plan(key)
    key = jax.random.fold_in(key, 11)
    counts = jnp.sum((plan[None, :] == jnp.arange(EXPERTS, dtype=jnp.int32)[:, None]).astype(jnp.int32), axis=1)
    offsets = jax.random.randint(key, (EXPERTS,), 0, 1 << 20)
    source_index = jnp.arange(N_EP, dtype=jnp.int32)[:, None]
    return ((source_index + offsets[None, :]) % counts[None, :]).astype(jnp.int32)


def draw_down_weight(key, part):
    plan = slot_plan(key)
    key = jax.random.fold_in(key, 23)
    base = jax.random.normal(key, (EXPERTS, F, D), jnp.float32) / F ** 0.5
    return base[plan].astype(jnp.bfloat16)


def block_levels(own_key, shape, cuts, least, top_value):
    loudness = 1.0
    for dim, parts in cuts:
        steps = jax.random.uniform(jax.random.fold_in(jax.random.fold_in(own_key, 6), dim), (parts,), jnp.float32, least / len(cuts), top_value / len(cuts))
        loudness = loudness * jnp.repeat(jnp.exp(steps), shape[dim] // parts).reshape((-1,) + (1,) * (len(shape) - 1 - dim))
    return loudness


def routed_block(stream_key, own, number, rows, amount, top, reach, slope):
    ranking = jax.random.permutation(stream_key, amount)
    crowded, ordinary = portions_of(amount, rows * top, reach, slope, True), portions_of(amount, rows * top, reach, slope, False)
    places = jnp.arange(amount)

    def named(lengths, turn):
        used = int((lengths > 0).sum())
        fixed = max(1, used // 4)
        passed = fixed + (places - fixed + turn * (used - fixed)) % max(1, amount - fixed)
        return jnp.zeros((amount,), jnp.int32).at[ranking[jnp.where(places < fixed, places, passed)]].set(jnp.asarray(lengths, jnp.int32))

    lengths = jnp.where(number % 4 == 0, named(crowded, number // 4), named(ordinary, number - number // 4 - 1))
    mixed = jax.random.permutation(jax.random.fold_in(own, 3), amount)
    donor, receiver = mixed[0:amount // 2 * 2:2], mixed[1:amount // 2 * 2:2]
    slack = jnp.minimum(lengths[donor] - 1, reach - lengths[receiver]) // 2
    slack = jnp.where((donor == ranking[0]) | (receiver == ranking[0]) | (lengths[receiver] == 0), 0, jnp.maximum(slack, 0))
    passed = jax.random.randint(jax.random.fold_in(own, 4), (amount // 2,), 0, 1 << 20) % (slack + 1)
    lengths = lengths.at[donor].add(-passed).at[receiver].add(passed)
    members = jnp.searchsorted(jnp.cumsum(lengths), jnp.arange(rows * top), side="right").astype(jnp.int32)
    table = members.reshape(top, rows).T
    table = table[jax.random.permutation(jax.random.fold_in(own, 1), rows)]
    turn = jax.random.randint(jax.random.fold_in(own, 2), (rows, 1), 0, top)
    return jnp.take_along_axis(table, (jnp.arange(top)[None, :] + turn) % top, axis=1)


def portions_of(amount, total, most, skew, full):
    loads = [(1 << 20) // math.isqrt(standing ** skew) + 1 for standing in range(1, amount + 1)]
    largest = most if full else min(most, max(-(-total // amount), total * loads[0] // sum(loads)))
    least = 1 if total - largest >= amount - 1 else 0
    given, surplus = [largest] + [least] * (amount - 1), total - largest - least * (amount - 1)
    while surplus > 0:
        movable = [i for i in range(1, amount) if given[i] < largest] or [i for i in range(1, amount) if given[i] < most]
        whole, left = sum([loads[i] for i in movable]), surplus
        for i in movable:
            more = min(most - given[i], max(1, left * loads[i] // whole), surplus)
            given[i] = given[i] + more
            surplus = surplus - more
    return np.array(given)


def centred(stream_key, shape, deviation, limit, shards=(), held_as=jnp.bfloat16):
    factor_of = block_levels(stream_key, shape, shards, -0.22, 0.18) if shards else 1.0
    array = jax.random.normal(stream_key, shape, jnp.float32) * deviation * factor_of
    return jnp.minimum(jnp.maximum(array, -limit), limit).astype(held_as)


def setup_inputs(seed: int = 0) -> dict:
    seeds = jax.random.split(jax.random.key(seed), 8)
    out_grad = centred(seeds[0], (TOKENS, D), 0.05, 0.3984375, ((0, 128), (1, 4)))
    route_weight = jnp.clip(jnp.exp(math.log(0.5) - 2.3025851 * jax.random.uniform(seeds[1], (TOKENS, TOPK), jnp.float32) ** block_levels(seeds[1], (TOKENS, TOPK), ((0, 128),), -0.2, 0.2)), 0.05, 0.5)
    expert_ids_keys = jax.random.split(jax.random.fold_in(seeds[2], 1), TOKENS // TOK_DEV)
    expert_ids_turns = jax.random.permutation(jax.random.fold_in(seeds[2], 3), TOKENS // TOK_DEV)
    expert_ids = jax.vmap(lambda own, number: routed_block(jax.random.fold_in(seeds[2], 2), own, number, TOK_DEV, EXPERTS, TOPK, PAIR, 2))(expert_ids_keys, expert_ids_turns).reshape((TOKENS, TOPK))
    slot_expert = draw_slot_expert(jax.random.fold_in(seeds[7], 71), 0)
    replica_pick = draw_replica_pick(jax.random.fold_in(seeds[7], 71), 0)
    saved_gu = centred(seeds[5], (SLOTS, ROWS_SLOT, 2, F), 1.0, 6.0, ((0, 128), (3, 4)))
    down_weight = draw_down_weight(jax.random.fold_in(seeds[7], 71), 0)
    return {"out_grad": out_grad, "route_weight": route_weight, "expert_ids": expert_ids, "slot_expert": slot_expert, "replica_pick": replica_pick, "saved_gu": saved_gu, "down_weight": down_weight}


def slot_ranking(slot_expert):
    slot_index = jnp.arange(slot_expert.shape[0], dtype=jnp.int32)
    same_expert = slot_expert[:, None] == slot_expert[None, :]
    earlier = slot_index[None, :] < slot_index[:, None]
    return jnp.sum((same_expert & earlier).astype(jnp.int32), axis=1).astype(jnp.int32)


def reference(out_grad, route_weight, expert_ids, slot_expert, replica_pick, saved_gu, down_weight):
    token_total = out_grad.shape[0]
    sources = replica_pick.shape[0]
    token_count = token_total // sources
    rows_total = saved_gu.shape[1]
    pair_rows = rows_total // sources
    copy_rank = slot_ranking(slot_expert)
    source_of = jnp.arange(token_total, dtype=jnp.int32) // token_count
    chosen_copy = replica_pick[source_of[:, None], expert_ids]
    matched = (slot_expert[None, None, :] == expert_ids[:, :, None]) & (copy_rank[None, None, :] == chosen_copy[:, :, None])
    slot_index = jnp.arange(SLOTS, dtype=jnp.int32)
    route_slot = jnp.sum(jnp.where(matched, slot_index, 0), axis=2).astype(jnp.int32)
    grouped = expert_ids.reshape(sources, token_count * TOPK)
    onehot = (grouped[:, :, None] == jnp.arange(EXPERTS, dtype=jnp.int32)).astype(jnp.int32)
    before = jnp.cumsum(onehot, axis=1) - onehot
    position = jnp.sum(before * onehot, axis=2).reshape(token_total, TOPK).astype(jnp.int32)
    row_index = source_of[:, None] * pair_rows + position
    flat_index = (route_slot * rows_total + row_index).reshape(-1).astype(jnp.int32)
    route_total = token_total * TOPK
    holder = jnp.full((SLOTS * rows_total,), -1, jnp.int32).at[flat_index].set(jnp.arange(route_total, dtype=jnp.int32))
    holder = holder.reshape(SLOTS, rows_total)
    weight_half = route_weight.astype(jnp.bfloat16).reshape(-1)

    def per_slot(leftover, inputs):
        preact, weight, row_holder = inputs
        filled = row_holder >= 0
        picked = jnp.where(filled, row_holder, 0).astype(jnp.int32)
        grad_rows = jnp.where(filled[:, None], out_grad[picked // TOPK], jnp.zeros((), out_grad.dtype))
        weights = jnp.where(filled, weight_half[picked].astype(jnp.float32), jnp.zeros((), jnp.float32))
        values = preact.astype(jnp.float32)
        hidden = (jax.nn.silu(values[:, 0]) * values[:, 1]).astype(jnp.bfloat16)
        hidden_wide = hidden.astype(jnp.float32)
        expert_out = jnp.dot(hidden_wide, weight.astype(jnp.float32), precision=lax.Precision.HIGHEST)
        route_dot = jnp.sum(grad_rows.astype(jnp.float32) * expert_out, axis=1)
        scaled = (weights[:, None] * grad_rows.astype(jnp.float32)).astype(jnp.bfloat16)
        partial_value = jnp.dot(hidden_wide.T, scaled.astype(jnp.float32), precision=lax.Precision.HIGHEST).astype(jnp.bfloat16)
        return leftover, (route_dot, partial_value)

    leftover, outputs = lax.scan(per_slot, jnp.zeros((), jnp.float32), (saved_gu, down_weight, holder))
    route_dots, partials = outputs
    route_grad = route_dots.reshape(-1)[flat_index].reshape(token_total, TOPK)
    blocks = 8
    block_rows = F // blocks
    stacked = jnp.moveaxis(partials.reshape(SLOTS, blocks, block_rows, D), 1, 0)

    def set_total(block):
        totals = jax.ops.segment_sum(block.astype(jnp.float32), slot_expert, num_segments=EXPERTS)
        return totals[slot_expert].astype(jnp.bfloat16)

    summed = lax.map(set_total, stacked)
    down_grad = jnp.moveaxis(summed, 0, 1).reshape(SLOTS, F, D)
    return down_grad, route_grad
```

```python
import jax
import jax.numpy as jnp
from jax import lax
from jax.experimental import pallas as pl
from jax.experimental.pallas import tpu as pltpu
from jax.sharding import PartitionSpec as P


def pack_kernel(ids_ref, weight_ref, slot_expert_ref, pick_ref, grad_ref, rows_ref, target_ref):
    top, tokens = ids_ref.shape
    experts = pick_ref.shape[1]
    slots = slot_expert_ref.shape[1]
    pair_rows = rows_ref.shape[0] // slots
    slot_expert = slot_expert_ref[...]
    lane = lax.broadcasted_iota(jnp.int32, (1, slots), 1)
    twin = pltpu.roll(slot_expert, slots // 2, 1)
    rank = jnp.where((lane >= slots // 2) & (twin == slot_expert), 1.0, 0.0)
    holds = lax.broadcasted_iota(jnp.int32, (experts, slots), 0) == slot_expert
    pick = jnp.dot(
        pick_ref[...].astype(jnp.bfloat16),
        jnp.where(holds, 1.0, 0.0).astype(jnp.bfloat16),
        preferred_element_type=jnp.float32,
    )
    serves = holds & (pick == rank)
    slot_of = jnp.sum(jnp.where(serves, lane, 0).astype(jnp.float32), axis=1, keepdims=True)
    expert = lax.broadcasted_iota(jnp.int32, (experts, tokens), 0)
    chosen = [expert == ids_ref[k : k + 1, :] for k in range(top)]
    named = sum(jnp.where(c, 1.0, 0.0) for c in chosen)
    earlier = lax.broadcasted_iota(jnp.int32, (tokens, tokens), 0) < lax.broadcasted_iota(
        jnp.int32, (tokens, tokens), 1
    )
    before = jnp.dot(
        named.astype(jnp.bfloat16),
        jnp.where(earlier, 1.0, 0.0).astype(jnp.bfloat16),
        preferred_element_type=jnp.float32,
    )
    place = slot_of * pair_rows + before
    row = lax.broadcasted_iota(jnp.int32, (slots * pair_rows, tokens), 0)
    mix = jnp.zeros((slots * pair_rows, tokens), jnp.float32)
    for k in range(top):
        target = jnp.sum(jnp.where(chosen[k], place, 0.0), axis=0, keepdims=True).astype(jnp.int32)
        target_ref[k : k + 1, :] = target
        mix += jnp.where(row == target, weight_ref[k : k + 1, :], 0.0)
    rows_ref[...] = jnp.dot(
        mix.astype(jnp.bfloat16), grad_ref[...], preferred_element_type=jnp.float32
    ).astype(rows_ref.dtype)


def pick_kernel(returned_ref, target_ref, weight_ref, out_ref):
    top, tokens = target_ref.shape
    slots, pair_rows = returned_ref.shape
    slot = lax.broadcasted_iota(jnp.int32, (slots, tokens), 0)
    for k in range(top):
        target = target_ref[k : k + 1, :]
        found = jnp.zeros((slots, tokens), jnp.float32)
        for p in range(pair_rows):
            found += jnp.where(slot * pair_rows + p == target, returned_ref[:, p : p + 1], 0.0)
        weight = weight_ref[k : k + 1, :].astype(jnp.bfloat16).astype(jnp.float32)
        out_ref[k : k + 1, :] = jnp.sum(found, axis=0, keepdims=True) / weight


def grad_kernel(shared_ref, hidden_ref, twin_hidden_ref, rows_ref, twin_rows_ref, out_ref):
    over_rows = (((0,), (0,)), ((), ()))
    own = lax.dot_general(
        hidden_ref[...], rows_ref[...], over_rows, preferred_element_type=jnp.float32
    )
    twin_rows = jnp.where(shared_ref[0, 0] > 0, twin_rows_ref[...], jnp.zeros((), jnp.bfloat16))
    twin = lax.dot_general(
        twin_hidden_ref[...], twin_rows, over_rows, preferred_element_type=jnp.float32
    )
    out_ref[...] = (own + twin).astype(out_ref.dtype)


def on_device(out_grad, route_weight, expert_ids, slot_expert, replica_pick, saved_gu, down_weight):
    sources = lax.axis_size("ep")
    token_count, top_count = expert_ids.shape
    slot_count = slot_expert.shape[0]
    rows_total = saved_gu.shape[1]
    pair_rows = rows_total // sources
    features = out_grad.shape[1]
    hidden_units = down_weight.shape[1]
    half = slot_count // 2
    swap = [(i, (i + half) % slot_count) for i in range(slot_count)]
    ids_t = expert_ids.T
    weight_t = route_weight.T
    send_rows, target = pl.pallas_call(
        pack_kernel,
        out_shape=(
            jax.ShapeDtypeStruct((rows_total, features), jnp.bfloat16),
            jax.ShapeDtypeStruct((top_count, token_count), jnp.int32),
        ),
        name="pack",
    )(ids_t, weight_t, slot_expert[None], replica_pick, out_grad)
    arrived = lax.all_to_all(
        send_rows.reshape(slot_count, pair_rows, features),
        "ep",
        split_axis=0,
        concat_axis=0,
        tiled=True,
    )
    values = saved_gu[0].astype(jnp.float32)
    part = (jax.nn.silu(values[:, 0]) * values[:, 1]).astype(jnp.bfloat16)
    twin_part = lax.ppermute(part, "ep", swap)
    hidden = lax.all_gather(part, "rep", axis=1, tiled=True)
    twin_hidden = lax.all_gather(twin_part, "rep", axis=1, tiled=True)
    outputs = jnp.dot(hidden, down_weight[0], preferred_element_type=jnp.float32)
    dots = jnp.sum(
        arrived.astype(jnp.float32) * outputs.reshape(sources, pair_rows, features), axis=2
    )
    dots = lax.psum(dots, "rep")
    returned = lax.all_to_all(
        dots.reshape(sources, 1, pair_rows), "ep", split_axis=0, concat_axis=0, tiled=True
    )
    route_grad = pl.pallas_call(
        pick_kernel,
        out_shape=jax.ShapeDtypeStruct((top_count, token_count), jnp.float32),
        name="pick",
    )(returned.reshape(slot_count, pair_rows), target, weight_t).T
    rows = arrived.reshape(rows_total, features)
    twin_rows = lax.ppermute(rows, "ep", swap)
    me = lax.axis_index("ep")
    own_expert = lax.dynamic_slice(slot_expert, (me,), (1,))
    twin_expert = lax.dynamic_slice(slot_expert, ((me + half) % slot_count,), (1,))
    shared = (own_expert == twin_expert).astype(jnp.int32).reshape(1, 1)
    steps = 4
    block = hidden_units // steps
    down_grad = pl.pallas_call(
        grad_kernel,
        grid=(steps,),
        in_specs=[
            pl.BlockSpec(memory_space=pltpu.SMEM),
            pl.BlockSpec((rows_total, block), lambda i: (0, i)),
            pl.BlockSpec((rows_total, block), lambda i: (0, i)),
            pl.BlockSpec((rows_total, features), lambda i: (0, 0)),
            pl.BlockSpec((rows_total, features), lambda i: (0, 0)),
        ],
        out_specs=pl.BlockSpec((block, features), lambda i: (i, 0)),
        out_shape=jax.ShapeDtypeStruct((hidden_units, features), jnp.bfloat16),
        cost_estimate=pl.CostEstimate(
            flops=4 * rows_total * hidden_units * features,
            bytes_accessed=4 * hidden_units * features,
            transcendentals=0,
        ),
        name="down_grad",
    )(shared, hidden, twin_hidden, rows, twin_rows)
    return (down_grad[None], route_grad)


def solution(mesh):
    placed = (
        P("ep", "rep"),
        P("ep", None),
        P("ep", None),
        P(),
        P("ep", None),
        P("ep", None, None, "rep"),
        P("ep", None, "rep"),
    )
    return jax.shard_map(
        on_device,
        mesh=mesh,
        in_specs=placed,
        out_specs=(P("ep", None, "rep"), P("ep", None)),
        check_vma=False,
    )
```

```python
import jax
import jax.numpy as jnp
from jax import lax
from jax.experimental import pallas as pl
from jax.experimental.pallas import tpu as pltpu
from jax.sharding import PartitionSpec as P


def pack_kernel(ids_ref, weight_ref, slot_expert_ref, pick_ref, grad_ref, rows_ref, target_ref):
    top, tokens = ids_ref.shape
    experts = pick_ref.shape[1]
    slots = slot_expert_ref.shape[1]
    pair_rows = rows_ref.shape[1]
    slot_expert = slot_expert_ref[...]
    lane = lax.broadcasted_iota(jnp.int32, (1, slots), 1)
    twin = pltpu.roll(slot_expert, slots // 2, 1)
    rank = jnp.where((lane >= slots // 2) & (twin == slot_expert), 1.0, 0.0)
    holds = lax.broadcasted_iota(jnp.int32, (experts, slots), 0) == slot_expert
    pick = jnp.dot(
        pick_ref[...].astype(jnp.bfloat16),
        jnp.where(holds, 1.0, 0.0).astype(jnp.bfloat16),
        preferred_element_type=jnp.float32,
    )
    serves = holds & (pick == rank)
    slot_of = jnp.sum(jnp.where(serves, lane, 0).astype(jnp.float32), axis=1, keepdims=True)
    expert = lax.broadcasted_iota(jnp.int32, (experts, tokens), 0)
    chosen = [expert == ids_ref[k : k + 1, :] for k in range(top)]
    named = sum(jnp.where(c, 1.0, 0.0) for c in chosen)
    earlier = lax.broadcasted_iota(jnp.int32, (tokens, tokens), 0) < lax.broadcasted_iota(
        jnp.int32, (tokens, tokens), 1
    )
    before = jnp.dot(
        named.astype(jnp.bfloat16),
        jnp.where(earlier, 1.0, 0.0).astype(jnp.bfloat16),
        preferred_element_type=jnp.float32,
    )
    place = slot_of * pair_rows + before
    row = lax.broadcasted_iota(jnp.int32, (slots * pair_rows, tokens), 0)
    mix = jnp.zeros((slots * pair_rows, tokens), jnp.float32)
    for k in range(top):
        target = jnp.sum(jnp.where(chosen[k], place, 0.0), axis=0, keepdims=True).astype(jnp.int32)
        target_ref[k : k + 1, :] = target
        mix += jnp.where(row == target, weight_ref[k : k + 1, :], 0.0)
    rows = jnp.dot(mix.astype(jnp.bfloat16), grad_ref[...], preferred_element_type=jnp.float32)
    rows_ref[...] = rows.astype(rows_ref.dtype).reshape(rows_ref.shape)


def hidden_kernel(saved_ref, out_ref):
    gate = saved_ref[:, 0, :].astype(jnp.float32)
    up = saved_ref[:, 1, :].astype(jnp.float32)
    out_ref[...] = (gate / (1.0 + jnp.exp(-gate)) * up).astype(out_ref.dtype)


def forward_kernel(hidden_ref, weight_ref, out_ref):
    out_ref[...] = jnp.dot(hidden_ref[...], weight_ref[...], preferred_element_type=jnp.float32)


def dots_kernel(arrived_ref, outputs_ref, _, dots_ref, scratch):
    rows = arrived_ref[...].reshape(outputs_ref.shape)
    total = jnp.sum(rows.astype(jnp.float32) * outputs_ref[...], axis=1, keepdims=True)
    scratch[...] = jnp.broadcast_to(total, scratch.shape)
    sources, pair_rows = dots_ref.shape
    lane = lax.broadcasted_iota(jnp.int32, (sources, scratch.shape[1]), 1)
    found = scratch[pl.ds(0, sources, stride=pair_rows), :]
    for p in range(1, pair_rows):
        found = jnp.where(lane == p, scratch[pl.ds(p, sources, stride=pair_rows), :], found)
    dots_ref[...] = found[:, :pair_rows]


def matrix_kernel(arrived_ref, _, rows_ref):
    rows_ref[...] = arrived_ref[...].reshape(rows_ref.shape)


def pick_kernel(returned_ref, target_ref, weight_ref, _, out_ref):
    top, tokens = target_ref.shape
    slots, pair_rows = returned_ref.shape
    slot = lax.broadcasted_iota(jnp.int32, (slots, tokens), 0)
    for k in range(top):
        target = target_ref[k : k + 1, :]
        found = jnp.zeros((slots, tokens), jnp.float32)
        for p in range(pair_rows):
            found += jnp.where(slot * pair_rows + p == target, returned_ref[:, p : p + 1], 0.0)
        weight = weight_ref[k : k + 1, :].astype(jnp.bfloat16).astype(jnp.float32)
        out_ref[k : k + 1, :] = jnp.sum(found, axis=0, keepdims=True) / weight


def grad_kernel(shared_ref, hidden_ref, twin_hidden_ref, rows_ref, twin_rows_ref, out_ref, order_ref):
    over_rows = (((0,), (0,)), ((), ()))
    own = lax.dot_general(
        hidden_ref[...], rows_ref[...], over_rows, preferred_element_type=jnp.float32
    )
    twin_rows = jnp.where(shared_ref[0, 0] > 0, twin_rows_ref[...], jnp.zeros((), jnp.bfloat16))
    twin = lax.dot_general(
        twin_hidden_ref[...], twin_rows, over_rows, preferred_element_type=jnp.float32
    )
    out_ref[...] = (own + twin).astype(out_ref.dtype)
    order_ref[...] = jnp.zeros_like(order_ref)


def on_device(out_grad, route_weight, expert_ids, slot_expert, replica_pick, saved_gu, down_weight):
    sources = lax.axis_size("ep")
    token_count, top_count = expert_ids.shape
    slot_count = slot_expert.shape[0]
    rows_total = saved_gu.shape[1]
    pair_rows = rows_total // sources
    features = out_grad.shape[1]
    hidden_units = down_weight.shape[1]
    half = slot_count // 2
    swap = [(i, (i + half) % slot_count) for i in range(slot_count)]
    ids_t = expert_ids.T
    weight_t = route_weight.T
    send_rows, target = pl.pallas_call(
        pack_kernel,
        out_shape=(
            jax.ShapeDtypeStruct((slot_count, pair_rows, features), jnp.bfloat16),
            jax.ShapeDtypeStruct((top_count, token_count), jnp.int32),
        ),
        name="pack",
    )(ids_t, weight_t, slot_expert[None], replica_pick, out_grad)
    arrived = lax.all_to_all(send_rows, "ep", split_axis=0, concat_axis=0, tiled=True)
    part = pl.pallas_call(
        hidden_kernel,
        out_shape=jax.ShapeDtypeStruct((rows_total, saved_gu.shape[3]), jnp.bfloat16),
        compiler_params=pltpu.CompilerParams(vmem_limit_bytes=8 << 20),
        name="hidden",
    )(saved_gu[0])
    twin_part = lax.ppermute(part, "ep", swap)
    hidden = lax.all_gather(part, "rep", axis=1, tiled=True)
    twin_hidden = lax.all_gather(twin_part, "rep", axis=1, tiled=True)
    outputs = pl.pallas_call(
        forward_kernel,
        out_shape=pltpu.VMEM((rows_total, features), jnp.float32),
        compiler_params=pltpu.CompilerParams(vmem_limit_bytes=12 << 20),
        name="forward",
    )(hidden, down_weight[0])
    dots = pl.pallas_call(
        dots_kernel,
        in_specs=[
            pl.BlockSpec(memory_space=pltpu.VMEM),
            pl.BlockSpec(memory_space=pltpu.VMEM),
            pl.BlockSpec(memory_space=pl.ANY),
        ],
        out_shape=jax.ShapeDtypeStruct((sources, pair_rows), jnp.float32),
        scratch_shapes=[pltpu.VMEM((rows_total, 128), jnp.float32)],
        compiler_params=pltpu.CompilerParams(vmem_limit_bytes=8 << 20),
        name="dots",
    )(arrived, outputs, twin_hidden)
    dots = lax.psum(dots, "rep")
    returned = lax.all_to_all(
        dots.reshape(sources, 1, pair_rows), "ep", split_axis=0, concat_axis=0, tiled=True
    )
    rows = pl.pallas_call(
        matrix_kernel,
        in_specs=[pl.BlockSpec(memory_space=pltpu.VMEM), pl.BlockSpec(memory_space=pl.ANY)],
        out_shape=jax.ShapeDtypeStruct((rows_total, features), jnp.bfloat16),
        compiler_params=pltpu.CompilerParams(vmem_limit_bytes=8 << 20),
        name="matrix",
    )(arrived, dots)
    twin_rows = lax.ppermute(rows, "ep", swap)
    me = lax.axis_index("ep")
    own_expert = lax.dynamic_slice(slot_expert, (me,), (1,))
    twin_expert = lax.dynamic_slice(slot_expert, ((me + half) % slot_count,), (1,))
    shared = (own_expert == twin_expert).astype(jnp.int32).reshape(1, 1)
    steps = 4
    block = hidden_units // steps
    down_grad, order = pl.pallas_call(
        grad_kernel,
        grid=(steps,),
        in_specs=[
            pl.BlockSpec(memory_space=pltpu.SMEM),
            pl.BlockSpec((rows_total, block), lambda i: (0, i)),
            pl.BlockSpec((rows_total, block), lambda i: (0, i)),
            pl.BlockSpec((rows_total, features), lambda i: (0, 0)),
            pl.BlockSpec((rows_total, features), lambda i: (0, 0)),
        ],
        out_specs=(
            pl.BlockSpec((block, features), lambda i: (i, 0)),
            pl.BlockSpec((8, 128), lambda i: (0, 0)),
        ),
        out_shape=(
            jax.ShapeDtypeStruct((hidden_units, features), jnp.bfloat16),
            jax.ShapeDtypeStruct((8, 128), jnp.float32),
        ),
        cost_estimate=pl.CostEstimate(
            flops=4 * rows_total * hidden_units * features,
            bytes_accessed=4 * hidden_units * features,
            transcendentals=0,
        ),
        compiler_params=pltpu.CompilerParams(vmem_limit_bytes=16 << 20),
        name="down_grad",
    )(shared, hidden, twin_hidden, rows, twin_rows)
    route_grad = pl.pallas_call(
        pick_kernel,
        in_specs=[pl.BlockSpec(memory_space=pltpu.VMEM)] * 3 + [pl.BlockSpec(memory_space=pl.ANY)],
        out_shape=jax.ShapeDtypeStruct((top_count, token_count), jnp.float32),
        compiler_params=pltpu.CompilerParams(vmem_limit_bytes=4 << 20),
        name="pick",
    )(returned.reshape(slot_count, pair_rows), target, weight_t, order).T
    return (down_grad[None], route_grad)


def solution(mesh):
    placed = (
        P("ep", "rep"),
        P("ep", None),
        P("ep", None),
        P(),
        P("ep", None),
        P("ep", None, None, "rep"),
        P("ep", None, "rep"),
    )
    return jax.shard_map(
        on_device,
        mesh=mesh,
        in_specs=placed,
        out_specs=(P("ep", None, "rep"), P("ep", None)),
        check_vma=False,
    )
```

```python
import jax
import jax.numpy as jnp
from jax import lax
from jax.experimental import pallas as pl
from jax.experimental.pallas import tpu as pltpu
from jax.sharding import PartitionSpec as P


def pack_kernel(ids_ref, weight_ref, slot_expert_ref, pick_ref, grad_ref, rows_ref, target_ref):
    top, tokens = ids_ref.shape
    experts = pick_ref.shape[1]
    slots = slot_expert_ref.shape[1]
    pair_rows = rows_ref.shape[1]
    slot_expert = slot_expert_ref[...]
    lane = lax.broadcasted_iota(jnp.int32, (1, slots), 1)
    twin = pltpu.roll(slot_expert, slots // 2, 1)
    rank = jnp.where((lane >= slots // 2) & (twin == slot_expert), 1.0, 0.0)
    holds = lax.broadcasted_iota(jnp.int32, (experts, slots), 0) == slot_expert
    pick = jnp.dot(
        pick_ref[...].astype(jnp.bfloat16),
        jnp.where(holds, 1.0, 0.0).astype(jnp.bfloat16),
        preferred_element_type=jnp.float32,
    )
    serves = holds & (pick == rank)
    slot_of = jnp.sum(jnp.where(serves, lane, 0).astype(jnp.float32), axis=1, keepdims=True)
    expert = lax.broadcasted_iota(jnp.int32, (experts, tokens), 0)
    chosen = [expert == ids_ref[k : k + 1, :] for k in range(top)]
    named = sum(jnp.where(c, 1.0, 0.0) for c in chosen)
    earlier = lax.broadcasted_iota(jnp.int32, (tokens, tokens), 0) < lax.broadcasted_iota(
        jnp.int32, (tokens, tokens), 1
    )
    before = jnp.dot(
        named.astype(jnp.bfloat16),
        jnp.where(earlier, 1.0, 0.0).astype(jnp.bfloat16),
        preferred_element_type=jnp.float32,
    )
    place = slot_of * pair_rows + before
    row = lax.broadcasted_iota(jnp.int32, (slots * pair_rows, tokens), 0)
    mix = jnp.zeros((slots * pair_rows, tokens), jnp.float32)
    for k in range(top):
        target = jnp.sum(jnp.where(chosen[k], place, 0.0), axis=0, keepdims=True).astype(jnp.int32)
        target_ref[k : k + 1, :] = target
        mix += jnp.where(row == target, weight_ref[k : k + 1, :], 0.0)
    rows = jnp.dot(mix.astype(jnp.bfloat16), grad_ref[...], preferred_element_type=jnp.float32)
    rows_ref[...] = rows.astype(rows_ref.dtype).reshape(rows_ref.shape)


def hidden_kernel(saved_ref, out_ref):
    gate = saved_ref[:, 0, :].astype(jnp.float32)
    up = saved_ref[:, 1, :].astype(jnp.float32)
    out_ref[...] = (gate / (1.0 + jnp.exp(-gate)) * up).astype(out_ref.dtype)


def forward_kernel(hidden_ref, weight_ref, out_ref):
    out_ref[...] = jnp.dot(hidden_ref[...], weight_ref[...], preferred_element_type=jnp.float32)


def dots_kernel(arrived_ref, outputs_ref, _, dots_ref, scratch):
    rows = arrived_ref[...].reshape(outputs_ref.shape)
    total = jnp.sum(rows.astype(jnp.float32) * outputs_ref[...], axis=1, keepdims=True)
    scratch[...] = jnp.broadcast_to(total, scratch.shape)
    sources, pair_rows = dots_ref.shape
    lane = lax.broadcasted_iota(jnp.int32, (sources, scratch.shape[1]), 1)
    found = scratch[pl.ds(0, sources, stride=pair_rows), :]
    for p in range(1, pair_rows):
        found = jnp.where(lane == p, scratch[pl.ds(p, sources, stride=pair_rows), :], found)
    dots_ref[...] = found[:, :pair_rows]


def matrix_kernel(arrived_ref, _, rows_ref):
    rows_ref[...] = arrived_ref[...].reshape(rows_ref.shape)


def pick_kernel(returned_ref, target_ref, weight_ref, _, out_ref):
    top, tokens = target_ref.shape
    slots, pair_rows = returned_ref.shape
    slot = lax.broadcasted_iota(jnp.int32, (slots, tokens), 0)
    for k in range(top):
        target = target_ref[k : k + 1, :]
        found = jnp.zeros((slots, tokens), jnp.float32)
        for p in range(pair_rows):
            found += jnp.where(slot * pair_rows + p == target, returned_ref[:, p : p + 1], 0.0)
        weight = weight_ref[k : k + 1, :].astype(jnp.bfloat16).astype(jnp.float32)
        out_ref[k : k + 1, :] = jnp.sum(found, axis=0, keepdims=True) / weight


def grad_kernel(slot_expert_ref, hidden_ref, twin_hidden_ref, rows_ref, twin_rows_ref, out_ref, order_ref):
    over_rows = (((0,), (0,)), ((), ()))
    own = lax.dot_general(
        hidden_ref[...], rows_ref[...], over_rows, preferred_element_type=jnp.float32
    )
    me = lax.axis_index("ep")
    slots = slot_expert_ref.shape[0]
    shared = slot_expert_ref[me] == slot_expert_ref[lax.rem(me + slots // 2, slots)]
    twin_rows = jnp.where(shared, twin_rows_ref[...], jnp.zeros((), jnp.bfloat16))
    twin = lax.dot_general(
        twin_hidden_ref[...], twin_rows, over_rows, preferred_element_type=jnp.float32
    )
    out_ref[...] = (own + twin).astype(out_ref.dtype)
    order_ref[...] = jnp.zeros_like(order_ref)


def on_device(out_grad, route_weight, expert_ids, slot_expert, replica_pick, saved_gu, down_weight):
    sources = lax.axis_size("ep")
    token_count, top_count = expert_ids.shape
    slot_count = slot_expert.shape[0]
    rows_total = saved_gu.shape[1]
    pair_rows = rows_total // sources
    features = out_grad.shape[1]
    hidden_units = down_weight.shape[1]
    half = slot_count // 2
    swap = [(i, (i + half) % slot_count) for i in range(slot_count)]
    ids_t = expert_ids.T
    weight_t = route_weight.T
    send_rows, target = pl.pallas_call(
        pack_kernel,
        out_shape=(
            jax.ShapeDtypeStruct((slot_count, pair_rows, features), jnp.bfloat16),
            jax.ShapeDtypeStruct((top_count, token_count), jnp.int32),
        ),
        name="pack",
    )(ids_t, weight_t, slot_expert[None], replica_pick, out_grad)
    arrived = lax.all_to_all(send_rows, "ep", split_axis=0, concat_axis=0, tiled=True)
    part = pl.pallas_call(
        hidden_kernel,
        out_shape=jax.ShapeDtypeStruct((rows_total, saved_gu.shape[3]), jnp.bfloat16),
        compiler_params=pltpu.CompilerParams(vmem_limit_bytes=8 << 20),
        name="hidden",
    )(saved_gu[0])
    twin_part = lax.ppermute(part, "ep", swap)
    hidden = lax.all_gather(part, "rep", axis=1, tiled=True)
    twin_hidden = lax.all_gather(twin_part, "rep", axis=1, tiled=True)
    outputs = pl.pallas_call(
        forward_kernel,
        out_shape=pltpu.VMEM((rows_total, features), jnp.float32),
        compiler_params=pltpu.CompilerParams(vmem_limit_bytes=12 << 20),
        name="forward",
    )(hidden, down_weight[0])
    dots = pl.pallas_call(
        dots_kernel,
        in_specs=[
            pl.BlockSpec(memory_space=pltpu.VMEM),
            pl.BlockSpec(memory_space=pltpu.VMEM),
            pl.BlockSpec(memory_space=pl.ANY),
        ],
        out_shape=jax.ShapeDtypeStruct((sources, pair_rows), jnp.float32),
        scratch_shapes=[pltpu.VMEM((rows_total, 128), jnp.float32)],
        compiler_params=pltpu.CompilerParams(vmem_limit_bytes=8 << 20),
        name="dots",
    )(arrived, outputs, twin_hidden)
    returned = lax.all_to_all(
        dots.reshape(sources, 1, pair_rows), "ep", split_axis=0, concat_axis=0, tiled=True
    )
    rows = pl.pallas_call(
        matrix_kernel,
        in_specs=[pl.BlockSpec(memory_space=pltpu.VMEM), pl.BlockSpec(memory_space=pl.ANY)],
        out_shape=jax.ShapeDtypeStruct((rows_total, features), jnp.bfloat16),
        compiler_params=pltpu.CompilerParams(vmem_limit_bytes=8 << 20),
        name="matrix",
    )(arrived, dots)
    twin_rows = lax.ppermute(rows, "ep", swap)
    steps = 4
    block = hidden_units // steps
    down_grad, order = pl.pallas_call(
        grad_kernel,
        grid=(steps,),
        in_specs=[
            pl.BlockSpec(memory_space=pltpu.SMEM),
            pl.BlockSpec((rows_total, block), lambda i: (0, i)),
            pl.BlockSpec((rows_total, block), lambda i: (0, i)),
            pl.BlockSpec((rows_total, features), lambda i: (0, 0)),
            pl.BlockSpec((rows_total, features), lambda i: (0, 0)),
        ],
        out_specs=(
            pl.BlockSpec((block, features), lambda i: (i, 0)),
            pl.BlockSpec((8, 128), lambda i: (0, 0)),
        ),
        out_shape=(
            jax.ShapeDtypeStruct((hidden_units, features), jnp.bfloat16),
            jax.ShapeDtypeStruct((8, 128), jnp.float32),
        ),
        compiler_params=pltpu.CompilerParams(vmem_limit_bytes=16 << 20),
        name="down_grad",
    )(slot_expert, hidden, twin_hidden, rows, twin_rows)
    route_part = pl.pallas_call(
        pick_kernel,
        in_specs=[pl.BlockSpec(memory_space=pltpu.VMEM)] * 3 + [pl.BlockSpec(memory_space=pl.ANY)],
        out_shape=jax.ShapeDtypeStruct((top_count, token_count), jnp.float32),
        compiler_params=pltpu.CompilerParams(vmem_limit_bytes=4 << 20),
        name="pick",
    )(returned.reshape(slot_count, pair_rows), target, weight_t, order)
    return (down_grad[None], lax.psum(route_part, "rep").T)


def solution(mesh):
    placed = (
        P("ep", "rep"),
        P("ep", None),
        P("ep", None),
        P(),
        P("ep", None),
        P("ep", None, None, "rep"),
        P("ep", None, "rep"),
    )
    return jax.shard_map(
        on_device,
        mesh=mesh,
        in_specs=placed,
        out_specs=(P("ep", None, "rep"), P("ep", None)),
        check_vma=False,
    )
```

```python
import jax
import jax.numpy as jnp
from jax import lax
from jax.experimental import pallas as pl
from jax.experimental.pallas import tpu as pltpu
from jax.sharding import Mesh, PartitionSpec as P


def prepare_kernel(
    ids_ref, weight_ref, slot_expert_ref, pick_ref, grad_ref, saved_ref, rows_ref, target_ref, hidden_ref
):
    gate = saved_ref[:, 0, :].astype(jnp.float32)
    up = saved_ref[:, 1, :].astype(jnp.float32)
    hidden_ref[...] = (gate / (1.0 + jnp.exp(-gate)) * up).astype(hidden_ref.dtype)
    top, tokens = ids_ref.shape
    experts = pick_ref.shape[1]
    slots = slot_expert_ref.shape[1]
    pair_rows = rows_ref.shape[1]
    slot_expert = slot_expert_ref[...]
    lane = lax.broadcasted_iota(jnp.int32, (1, slots), 1)
    twin = pltpu.roll(slot_expert, slots // 2, 1)
    rank = jnp.where((lane >= slots // 2) & (twin == slot_expert), 1.0, 0.0)
    holds = lax.broadcasted_iota(jnp.int32, (experts, slots), 0) == slot_expert
    pick = jnp.dot(
        pick_ref[...].astype(jnp.bfloat16),
        jnp.where(holds, 1.0, 0.0).astype(jnp.bfloat16),
        preferred_element_type=jnp.float32,
    )
    serves = holds & (pick == rank)
    slot_of = jnp.sum(jnp.where(serves, lane, 0).astype(jnp.float32), axis=1, keepdims=True)
    expert = lax.broadcasted_iota(jnp.int32, (experts, tokens), 0)
    chosen = [expert == ids_ref[k : k + 1, :] for k in range(top)]
    named = sum(jnp.where(c, 1.0, 0.0) for c in chosen)
    earlier = lax.broadcasted_iota(jnp.int32, (tokens, tokens), 0) < lax.broadcasted_iota(
        jnp.int32, (tokens, tokens), 1
    )
    before = jnp.dot(
        named.astype(jnp.bfloat16),
        jnp.where(earlier, 1.0, 0.0).astype(jnp.bfloat16),
        preferred_element_type=jnp.float32,
    )
    place = slot_of * pair_rows + before
    row = lax.broadcasted_iota(jnp.int32, (slots * pair_rows, tokens), 0)
    mix = jnp.zeros((slots * pair_rows, tokens), jnp.float32)
    for k in range(top):
        target = jnp.sum(jnp.where(chosen[k], place, 0.0), axis=0, keepdims=True).astype(jnp.int32)
        target_ref[k : k + 1, :] = target
        mix += jnp.where(row == target, weight_ref[k : k + 1, :], 0.0)
    rows = jnp.dot(mix.astype(jnp.bfloat16), grad_ref[...], preferred_element_type=jnp.float32)
    rows_ref[...] = rows.astype(rows_ref.dtype).reshape(rows_ref.shape)


def forward_kernel(hidden_ref, weight_ref, out_ref):
    units = weight_ref.shape[0]
    own = pl.multiple_of(lax.axis_index("half") * units, units)
    out_ref[...] = jnp.dot(
        hidden_ref[:, pl.ds(own, units)], weight_ref[...], preferred_element_type=jnp.float32
    )


def dots_kernel(arrived_ref, outputs_ref, dots_ref, scratch):
    rows = arrived_ref[...].reshape(outputs_ref.shape)
    total = jnp.sum(rows.astype(jnp.float32) * outputs_ref[...], axis=1, keepdims=True)
    scratch[...] = jnp.broadcast_to(total, scratch.shape)
    sources, pair_rows = dots_ref.shape
    lane = lax.broadcasted_iota(jnp.int32, (sources, scratch.shape[1]), 1)
    found = scratch[pl.ds(0, sources, stride=pair_rows), :]
    for p in range(1, pair_rows):
        found = jnp.where(lane == p, scratch[pl.ds(p, sources, stride=pair_rows), :], found)
    dots_ref[...] = found[:, :pair_rows]


def matrix_kernel(arrived_ref, _, rows_ref):
    rows_ref[...] = arrived_ref[...].reshape(rows_ref.shape)


def pick_kernel(returned_ref, target_ref, weight_ref, _, out_ref):
    top, tokens = target_ref.shape
    slots, pair_rows = returned_ref.shape
    slot = lax.broadcasted_iota(jnp.int32, (slots, tokens), 0)
    for k in range(top):
        target = target_ref[k : k + 1, :]
        found = jnp.zeros((slots, tokens), jnp.float32)
        for p in range(pair_rows):
            found += jnp.where(slot * pair_rows + p == target, returned_ref[:, p : p + 1], 0.0)
        weight = weight_ref[k : k + 1, :].astype(jnp.bfloat16).astype(jnp.float32)
        out_ref[k : k + 1, :] = jnp.sum(found, axis=0, keepdims=True) / weight


def grad_kernel(slot_expert_ref, hidden_ref, twin_hidden_ref, rows_ref, out_ref, order_ref):
    over_rows = (((0,), (0,)), ((), ()))
    half = lax.axis_index("half")
    place = lax.axis_index("place")
    shared = slot_expert_ref[place] == slot_expert_ref[place + slot_expert_ref.shape[0] // 2]
    count = hidden_ref.shape[0]
    total = jnp.zeros(out_ref.shape, jnp.float32)
    for part, ref in enumerate((hidden_ref, twin_hidden_ref)):
        rows = rows_ref[part * count : (part + 1) * count, :]
        rows = jnp.where(shared | (half == part), rows, jnp.zeros((), rows.dtype))
        total += lax.dot_general(ref[...], rows, over_rows, preferred_element_type=jnp.float32)
    out_ref[...] = total.astype(out_ref.dtype)
    order_ref[...] = jnp.zeros_like(order_ref)


def on_device(out_grad, route_weight, expert_ids, slot_expert, replica_pick, saved_gu, down_weight):
    ep = ("half", "place")
    sources = lax.axis_size(ep)
    token_count, top_count = expert_ids.shape
    slot_count = slot_expert.shape[0]
    rows_total = saved_gu.shape[1]
    pair_rows = rows_total // sources
    features = out_grad.shape[1]
    hidden_units = down_weight.shape[1]
    ids_t = expert_ids.T
    weight_t = route_weight.T
    send_rows, target, part = pl.pallas_call(
        prepare_kernel,
        out_shape=(
            jax.ShapeDtypeStruct((slot_count, pair_rows, features), jnp.bfloat16),
            jax.ShapeDtypeStruct((top_count, token_count), jnp.int32),
            jax.ShapeDtypeStruct((rows_total, saved_gu.shape[3]), jnp.bfloat16),
        ),

        name="prepare",
    )(ids_t, weight_t, slot_expert[None], replica_pick, out_grad, saved_gu[0])
    arrived = lax.all_to_all(send_rows, ep, split_axis=0, concat_axis=0, tiled=True)
    hidden = lax.all_gather(part, ("half", "rep"), axis=1, tiled=True)
    outputs = pl.pallas_call(
        forward_kernel,
        out_shape=pltpu.VMEM((rows_total, features), jnp.float32),
        compiler_params=pltpu.CompilerParams(vmem_limit_bytes=12 << 20),
        name="forward",
    )(hidden, down_weight[0])
    dots = pl.pallas_call(
        dots_kernel,
        in_specs=[pl.BlockSpec(memory_space=pltpu.VMEM)] * 2,
        out_shape=jax.ShapeDtypeStruct((sources, pair_rows), jnp.float32),
        scratch_shapes=[pltpu.VMEM((rows_total, 128), jnp.float32)],
        compiler_params=pltpu.CompilerParams(vmem_limit_bytes=8 << 20),
        name="dots",
    )(arrived, outputs)
    returned = lax.all_to_all(
        dots.reshape(sources, 1, pair_rows), ep, split_axis=0, concat_axis=0, tiled=True
    )
    rows = pl.pallas_call(
        matrix_kernel,
        in_specs=[pl.BlockSpec(memory_space=pltpu.VMEM), pl.BlockSpec(memory_space=pl.ANY)],
        out_shape=jax.ShapeDtypeStruct((rows_total, features), jnp.bfloat16),
        compiler_params=pltpu.CompilerParams(vmem_limit_bytes=8 << 20),
        name="matrix",
    )(arrived, dots)
    rows = lax.all_gather(rows, "half", axis=0, tiled=True)
    steps = 4
    block = hidden_units // steps
    down_grad, order = pl.pallas_call(
        grad_kernel,
        grid=(steps,),
        in_specs=[
            pl.BlockSpec(memory_space=pltpu.SMEM),
            pl.BlockSpec((rows_total, block), lambda i: (0, i)),
            pl.BlockSpec((rows_total, block), lambda i: (0, i + steps)),
            pl.BlockSpec((2 * rows_total, features), lambda i: (0, 0)),
        ],
        out_specs=(
            pl.BlockSpec((block, features), lambda i: (i, 0)),
            pl.BlockSpec((8, 128), lambda i: (0, 0)),
        ),
        out_shape=(
            jax.ShapeDtypeStruct((hidden_units, features), jnp.bfloat16),
            jax.ShapeDtypeStruct((8, 128), jnp.float32),
        ),
        compiler_params=pltpu.CompilerParams(vmem_limit_bytes=16 << 20),
        name="down_grad",
    )(slot_expert, hidden, hidden, rows)
    route_part = pl.pallas_call(
        pick_kernel,
        in_specs=[pl.BlockSpec(memory_space=pltpu.VMEM)] * 3 + [pl.BlockSpec(memory_space=pl.ANY)],
        out_shape=jax.ShapeDtypeStruct((top_count, token_count), jnp.float32),
        compiler_params=pltpu.CompilerParams(vmem_limit_bytes=4 << 20),
        name="pick",
    )(returned.reshape(slot_count, pair_rows), target, weight_t, order)
    return (down_grad[None], lax.psum(route_part, "rep").T)


def solution(mesh):
    ep, rep = mesh.shape["ep"], mesh.shape["rep"]
    halves = Mesh(mesh.devices.reshape(2, ep // 2, rep), ("half", "place", "rep"))
    ep = ("half", "place")
    placed = (
        P(ep, "rep"),
        P(ep, None),
        P(ep, None),
        P(),
        P(ep, None),
        P(ep, None, None, "rep"),
        P(ep, None, "rep"),
    )
    return jax.shard_map(
        on_device,
        mesh=halves,
        in_specs=placed,
        out_specs=(P(ep, None, "rep"), P(ep, None)),
        check_vma=False,
    )
```

```python
import jax
import jax.numpy as jnp
from jax import lax
from jax.experimental import pallas as pl
from jax.experimental.pallas import tpu as pltpu
from jax.sharding import Mesh, PartitionSpec as P


def pack_kernel(ids_ref, weight_ref, slot_expert_ref, pick_ref, grad_ref, rows_ref, target_ref):
    top, tokens = ids_ref.shape
    experts = pick_ref.shape[1]
    slots = slot_expert_ref.shape[1]
    pair_rows = rows_ref.shape[1]
    slot_expert = slot_expert_ref[...]
    lane = lax.broadcasted_iota(jnp.int32, (1, slots), 1)
    twin = pltpu.roll(slot_expert, slots // 2, 1)
    rank = jnp.where((lane >= slots // 2) & (twin == slot_expert), 1.0, 0.0)
    holds = lax.broadcasted_iota(jnp.int32, (experts, slots), 0) == slot_expert
    pick = jnp.dot(
        pick_ref[...].astype(jnp.bfloat16),
        jnp.where(holds, 1.0, 0.0).astype(jnp.bfloat16),
        preferred_element_type=jnp.float32,
    )
    serves = holds & (pick == rank)
    slot_of = jnp.sum(jnp.where(serves, lane, 0).astype(jnp.float32), axis=1, keepdims=True)
    expert = lax.broadcasted_iota(jnp.int32, (experts, tokens), 0)
    chosen = [expert == ids_ref[k : k + 1, :] for k in range(top)]
    named = sum(jnp.where(c, 1.0, 0.0) for c in chosen)
    earlier = lax.broadcasted_iota(jnp.int32, (tokens, tokens), 0) < lax.broadcasted_iota(
        jnp.int32, (tokens, tokens), 1
    )
    before = jnp.dot(
        named.astype(jnp.bfloat16),
        jnp.where(earlier, 1.0, 0.0).astype(jnp.bfloat16),
        preferred_element_type=jnp.float32,
    )
    place = slot_of * pair_rows + before
    row = lax.broadcasted_iota(jnp.int32, (slots * pair_rows, tokens), 0)
    mix = jnp.zeros((slots * pair_rows, tokens), jnp.float32)
    for k in range(top):
        target = jnp.sum(jnp.where(chosen[k], place, 0.0), axis=0, keepdims=True).astype(jnp.int32)
        target_ref[k : k + 1, :] = target
        mix += jnp.where(row == target, weight_ref[k : k + 1, :], 0.0)
    rows = jnp.dot(mix.astype(jnp.bfloat16), grad_ref[...], preferred_element_type=jnp.float32)
    rows_ref[...] = rows.astype(rows_ref.dtype).reshape(rows_ref.shape)


def hidden_kernel(saved_ref, out_ref):
    gate = saved_ref[:, 0, :].astype(jnp.float32)
    up = saved_ref[:, 1, :].astype(jnp.float32)
    out_ref[...] = (gate / (1.0 + jnp.exp(-gate)) * up).astype(out_ref.dtype)


def forward_kernel(hidden_ref, weight_ref, out_ref):
    out_ref[...] = jnp.dot(hidden_ref[...], weight_ref[...], preferred_element_type=jnp.float32)


def dots_kernel(arrived_ref, outputs_ref, _, dots_ref, scratch):
    rows = arrived_ref[...].reshape(outputs_ref.shape)
    total = jnp.sum(rows.astype(jnp.float32) * outputs_ref[...], axis=1, keepdims=True)
    scratch[...] = jnp.broadcast_to(total, scratch.shape)
    sources, pair_rows = dots_ref.shape
    lane = lax.broadcasted_iota(jnp.int32, (sources, scratch.shape[1]), 1)
    found = scratch[pl.ds(0, sources, stride=pair_rows), :]
    for p in range(1, pair_rows):
        found = jnp.where(lane == p, scratch[pl.ds(p, sources, stride=pair_rows), :], found)
    dots_ref[...] = found[:, :pair_rows]


def matrix_kernel(arrived_ref, _, rows_ref):
    rows_ref[...] = arrived_ref[...].reshape(rows_ref.shape)


def pick_kernel(returned_ref, target_ref, weight_ref, _, out_ref):
    top, tokens = target_ref.shape
    slots, pair_rows = returned_ref.shape
    slot = lax.broadcasted_iota(jnp.int32, (slots, tokens), 0)
    for k in range(top):
        target = target_ref[k : k + 1, :]
        found = jnp.zeros((slots, tokens), jnp.float32)
        for p in range(pair_rows):
            found += jnp.where(slot * pair_rows + p == target, returned_ref[:, p : p + 1], 0.0)
        weight = weight_ref[k : k + 1, :].astype(jnp.bfloat16).astype(jnp.float32)
        out_ref[k : k + 1, :] = jnp.sum(found, axis=0, keepdims=True) / weight


def grad_kernel(slot_expert_ref, hidden_ref, twin_hidden_ref, rows_ref, out_ref, order_ref, used):
    over_rows = (((0,), (0,)), ((), ()))
    count = hidden_ref.shape[0]

    @pl.when(pl.program_id(0) == 0)
    def _():
        half = lax.axis_index("half")
        place = lax.axis_index("place")
        shared = slot_expert_ref[place] == slot_expert_ref[place + slot_expert_ref.shape[0] // 2]
        lower, upper = rows_ref[:count, :], rows_ref[count:, :]
        twin_rows = jnp.where(half == 0, upper, lower)
        used[:count, :] = jnp.where(half == 0, lower, upper)
        used[count:, :] = jnp.where(shared, twin_rows, jnp.zeros((), twin_rows.dtype))
        order_ref[...] = jnp.zeros_like(order_ref)

    own = lax.dot_general(
        hidden_ref[...], used[:count, :], over_rows, preferred_element_type=jnp.float32
    )
    twin = lax.dot_general(
        twin_hidden_ref[...], used[count:, :], over_rows, preferred_element_type=jnp.float32
    )
    out_ref[...] = (own + twin).astype(out_ref.dtype)


def on_device(out_grad, route_weight, expert_ids, slot_expert, replica_pick, saved_gu, down_weight):
    ep = ("half", "place")
    sources = lax.axis_size(ep)
    token_count, top_count = expert_ids.shape
    slot_count = slot_expert.shape[0]
    rows_total = saved_gu.shape[1]
    pair_rows = rows_total // sources
    features = out_grad.shape[1]
    hidden_units = down_weight.shape[1]
    ids_t = expert_ids.T
    weight_t = route_weight.T
    send_rows, target = pl.pallas_call(
        pack_kernel,
        out_shape=(
            jax.ShapeDtypeStruct((slot_count, pair_rows, features), jnp.bfloat16),
            jax.ShapeDtypeStruct((top_count, token_count), jnp.int32),
        ),
        name="pack",
    )(ids_t, weight_t, slot_expert[None], replica_pick, out_grad)
    arrived = lax.all_to_all(send_rows, ep, split_axis=0, concat_axis=0, tiled=True)
    part = pl.pallas_call(
        hidden_kernel,
        out_shape=jax.ShapeDtypeStruct((rows_total, saved_gu.shape[3]), jnp.bfloat16),
        compiler_params=pltpu.CompilerParams(vmem_limit_bytes=8 << 20),
        name="hidden",
    )(saved_gu[0])
    twin_part = lax.ppermute(part, "half", [(0, 1), (1, 0)])
    hidden = lax.all_gather(part, "rep", axis=1, tiled=True)
    twin_hidden = lax.all_gather(twin_part, "rep", axis=1, tiled=True)
    outputs = pl.pallas_call(
        forward_kernel,
        out_shape=pltpu.VMEM((rows_total, features), jnp.float32),
        compiler_params=pltpu.CompilerParams(vmem_limit_bytes=12 << 20),
        name="forward",
    )(hidden, down_weight[0])
    dots = pl.pallas_call(
        dots_kernel,
        in_specs=[pl.BlockSpec(memory_space=pltpu.VMEM)] * 2 + [pl.BlockSpec(memory_space=pl.ANY)],
        out_shape=jax.ShapeDtypeStruct((sources, pair_rows), jnp.float32),
        scratch_shapes=[pltpu.VMEM((rows_total, 128), jnp.float32)],
        compiler_params=pltpu.CompilerParams(vmem_limit_bytes=8 << 20),
        name="dots",
    )(arrived, outputs, twin_hidden)
    returned = lax.all_to_all(
        dots.reshape(sources, 1, pair_rows), ep, split_axis=0, concat_axis=0, tiled=True
    )
    rows = pl.pallas_call(
        matrix_kernel,
        in_specs=[pl.BlockSpec(memory_space=pltpu.VMEM), pl.BlockSpec(memory_space=pl.ANY)],
        out_shape=jax.ShapeDtypeStruct((rows_total, features), jnp.bfloat16),
        compiler_params=pltpu.CompilerParams(vmem_limit_bytes=8 << 20),
        name="matrix",
    )(arrived, dots)
    rows = lax.all_gather(rows, "half", axis=0, tiled=True)
    steps = 2
    block = hidden_units // steps
    down_grad, order = pl.pallas_call(
        grad_kernel,
        grid=(steps,),
        in_specs=[
            pl.BlockSpec(memory_space=pltpu.SMEM),
            pl.BlockSpec((rows_total, block), lambda i: (0, i)),
            pl.BlockSpec((rows_total, block), lambda i: (0, i)),
            pl.BlockSpec((2 * rows_total, features), lambda i: (0, 0)),
        ],
        out_specs=(
            pl.BlockSpec((block, features), lambda i: (i, 0)),
            pl.BlockSpec((8, 128), lambda i: (0, 0)),
        ),
        out_shape=(
            jax.ShapeDtypeStruct((hidden_units, features), jnp.bfloat16),
            jax.ShapeDtypeStruct((8, 128), jnp.float32),
        ),
        scratch_shapes=[pltpu.VMEM((2 * rows_total, features), jnp.bfloat16)],
        compiler_params=pltpu.CompilerParams(vmem_limit_bytes=24 << 20),
        name="down_grad",
    )(slot_expert, hidden, twin_hidden, rows)
    route_part = pl.pallas_call(
        pick_kernel,
        in_specs=[pl.BlockSpec(memory_space=pltpu.VMEM)] * 3 + [pl.BlockSpec(memory_space=pl.ANY)],
        out_shape=jax.ShapeDtypeStruct((top_count, token_count), jnp.float32),
        compiler_params=pltpu.CompilerParams(vmem_limit_bytes=4 << 20),
        name="pick",
    )(returned.reshape(slot_count, pair_rows), target, weight_t, order)
    return (down_grad[None], lax.psum(route_part, "rep").T)


def solution(mesh):
    ep, rep = mesh.shape["ep"], mesh.shape["rep"]
    halves = Mesh(mesh.devices.reshape(2, ep // 2, rep), ("half", "place", "rep"))
    ep = ("half", "place")
    placed = (
        P(ep, "rep"),
        P(ep, None),
        P(ep, None),
        P(),
        P(ep, None),
        P(ep, None, None, "rep"),
        P(ep, None, "rep"),
    )
    return jax.shard_map(
        on_device,
        mesh=halves,
        in_specs=placed,
        out_specs=(P(ep, None, "rep"), P(ep, None)),
        check_vma=False,
    )
```

```python
import jax
import jax.numpy as jnp
from jax import lax
from jax.experimental import pallas as pl
from jax.experimental.pallas import tpu as pltpu
from jax.sharding import Mesh, PartitionSpec as P


def pack_kernel(ids_ref, weight_ref, slot_expert_ref, pick_ref, grad_ref, rows_ref, target_ref):
    top, tokens = ids_ref.shape
    experts = pick_ref.shape[1]
    slots, pair_rows, _ = rows_ref.shape
    features = grad_ref.shape[1]
    slot_expert = slot_expert_ref[...]
    lane = lax.broadcasted_iota(jnp.int32, (1, slots), 1)
    twin = pltpu.roll(slot_expert, slots // 2, 1)
    shared = jnp.where(twin == slot_expert, 1, 0)
    rank = jnp.where((lane >= slots // 2) & (shared > 0), 1.0, 0.0)
    holds = lax.broadcasted_iota(jnp.int32, (experts, slots), 0) == slot_expert
    pick = jnp.dot(
        pick_ref[...].astype(jnp.bfloat16),
        jnp.where(holds, 1.0, 0.0).astype(jnp.bfloat16),
        preferred_element_type=jnp.float32,
    )
    picked = pick == rank
    serves = holds & picked
    slot_of = jnp.sum(jnp.where(serves, lane, 0).astype(jnp.float32), axis=1, keepdims=True)
    other = jnp.where(shared > 0, jnp.where(lane < slots // 2, slots // 2, -(slots // 2)), 0)
    twin_of = slot_of + jnp.sum(
        jnp.where(serves, other, 0).astype(jnp.float32), axis=1, keepdims=True
    )
    expert = lax.broadcasted_iota(jnp.int32, (experts, tokens), 0)
    chosen = [expert == ids_ref[k : k + 1, :] for k in range(top)]
    named = sum(jnp.where(c, 1.0, 0.0) for c in chosen)
    earlier = lax.broadcasted_iota(jnp.int32, (tokens, tokens), 0) < lax.broadcasted_iota(
        jnp.int32, (tokens, tokens), 1
    )
    before = jnp.dot(
        named.astype(jnp.bfloat16),
        jnp.where(earlier, 1.0, 0.0).astype(jnp.bfloat16),
        preferred_element_type=jnp.float32,
    )
    place = slot_of * pair_rows + before
    twin_place = twin_of * pair_rows + before
    row = lax.broadcasted_iota(jnp.int32, (slots * pair_rows, tokens), 0)
    mix = jnp.zeros((slots * pair_rows, tokens), jnp.float32)
    for k in range(top):
        target = jnp.sum(jnp.where(chosen[k], place, 0.0), axis=0, keepdims=True).astype(jnp.int32)
        twin_target = jnp.sum(jnp.where(chosen[k], twin_place, 0.0), axis=0, keepdims=True)
        target_ref[k : k + 1, :] = target
        here = (row == target) | (row == twin_target.astype(jnp.int32))
        mix += jnp.where(here, weight_ref[k : k + 1, :], 0.0)
    rows = jnp.dot(mix.astype(jnp.bfloat16), grad_ref[...], preferred_element_type=jnp.float32)
    rows_ref[:, :, :features] = rows.astype(rows_ref.dtype).reshape(slots, pair_rows, features)
    slot = lax.broadcasted_iota(jnp.int32, (slots * pair_rows, slots), 0) // pair_rows
    chosen_slot = (slot == lane) & picked
    rows_ref[:, :, features:] = (
        jnp.where(chosen_slot, 1.0, 0.0).astype(rows_ref.dtype).reshape(slots, pair_rows, slots)
    )


def hidden_kernel(saved_ref, out_ref):
    gate = saved_ref[:, 0, :].astype(jnp.float32)
    up = saved_ref[:, 1, :].astype(jnp.float32)
    out_ref[...] = (gate / (1.0 + jnp.exp(-gate)) * up).astype(out_ref.dtype)


def forward_kernel(hidden_ref, weight_ref, out_ref):
    out_ref[...] = jnp.dot(hidden_ref[...], weight_ref[...], preferred_element_type=jnp.float32)


def dots_kernel(arrived_ref, outputs_ref, dots_ref, scratch):
    rows = arrived_ref[:, :, : outputs_ref.shape[1]].reshape(outputs_ref.shape)
    total = jnp.sum(rows.astype(jnp.float32) * outputs_ref[...], axis=1, keepdims=True)
    scratch[...] = jnp.broadcast_to(total, scratch.shape)
    sources, pair_rows = dots_ref.shape
    lane = lax.broadcasted_iota(jnp.int32, (sources, scratch.shape[1]), 1)
    found = scratch[pl.ds(0, sources, stride=pair_rows), :]
    for p in range(1, pair_rows):
        found = jnp.where(lane == p, scratch[pl.ds(p, sources, stride=pair_rows), :], found)
    dots_ref[...] = found[:, :pair_rows]


def pick_kernel(returned_ref, target_ref, weight_ref, _, out_ref):
    top, tokens = target_ref.shape
    slots, pair_rows = returned_ref.shape
    slot = lax.broadcasted_iota(jnp.int32, (slots, tokens), 0)
    for k in range(top):
        target = target_ref[k : k + 1, :]
        found = jnp.zeros((slots, tokens), jnp.float32)
        for p in range(pair_rows):
            found += jnp.where(slot * pair_rows + p == target, returned_ref[:, p : p + 1], 0.0)
        weight = weight_ref[k : k + 1, :].astype(jnp.bfloat16).astype(jnp.float32)
        out_ref[k : k + 1, :] = jnp.sum(found, axis=0, keepdims=True) / weight


def grad_kernel(_, arrived_ref, hidden_ref, twin_hidden_ref, out_ref, order_ref, rows_ref, own_ref):
    features = out_ref.shape[1]
    rows = rows_ref.shape[0]

    @pl.when(pl.program_id(0) == 0)
    def _():
        rows_ref[...] = arrived_ref[:, :, :features].reshape(rows_ref.shape)
        picked = arrived_ref[:, :, features:].reshape(rows, arrived_ref.shape[2] - features)
        picked = jnp.sum(picked.astype(jnp.float32), axis=1, keepdims=True)
        own_ref[...] = jnp.broadcast_to(picked, own_ref.shape)
        order_ref[...] = jnp.zeros_like(order_ref)

    own = own_ref[:, :1] > 0.5
    hidden = jnp.where(own, hidden_ref[...], twin_hidden_ref[...])
    out_ref[...] = lax.dot_general(
        hidden, rows_ref[...], (((0,), (0,)), ((), ())), preferred_element_type=jnp.float32
    ).astype(out_ref.dtype)


def on_device(out_grad, route_weight, expert_ids, slot_expert, replica_pick, saved_gu, down_weight):
    ep = ("half", "place")
    sources = lax.axis_size(ep)
    token_count, top_count = expert_ids.shape
    slot_count = slot_expert.shape[0]
    rows_total = saved_gu.shape[1]
    pair_rows = rows_total // sources
    features = out_grad.shape[1]
    hidden_units = down_weight.shape[1]
    ids_t = expert_ids.T
    weight_t = route_weight.T
    send_rows, target = pl.pallas_call(
        pack_kernel,
        out_shape=(
            jax.ShapeDtypeStruct((slot_count, pair_rows, features + slot_count), jnp.bfloat16),
            jax.ShapeDtypeStruct((top_count, token_count), jnp.int32),
        ),
        name="pack",
    )(ids_t, weight_t, slot_expert[None], replica_pick, out_grad)
    arrived = lax.all_to_all(send_rows, ep, split_axis=0, concat_axis=0, tiled=True)
    part = pl.pallas_call(
        hidden_kernel,
        out_shape=jax.ShapeDtypeStruct((rows_total, saved_gu.shape[3]), jnp.bfloat16),
        compiler_params=pltpu.CompilerParams(vmem_limit_bytes=8 << 20),
        name="hidden",
    )(saved_gu[0])
    twin_part = lax.ppermute(part, "half", [(0, 1), (1, 0)])
    hidden = lax.all_gather(part, "rep", axis=1, tiled=True)
    twin_hidden = lax.all_gather(twin_part, "rep", axis=1, tiled=True)
    outputs = pl.pallas_call(
        forward_kernel,
        out_shape=pltpu.VMEM((rows_total, features), jnp.float32),
        compiler_params=pltpu.CompilerParams(vmem_limit_bytes=12 << 20),
        name="forward",
    )(hidden, down_weight[0])
    dots = pl.pallas_call(
        dots_kernel,
        in_specs=[pl.BlockSpec(memory_space=pltpu.VMEM)] * 2,
        out_shape=jax.ShapeDtypeStruct((sources, pair_rows), jnp.float32),
        scratch_shapes=[pltpu.VMEM((rows_total, 128), jnp.float32)],
        compiler_params=pltpu.CompilerParams(vmem_limit_bytes=8 << 20),
        name="dots",
    )(arrived, outputs)
    returned = lax.all_to_all(
        dots.reshape(sources, 1, pair_rows), ep, split_axis=0, concat_axis=0, tiled=True
    )
    steps = 2
    block = hidden_units // steps
    down_grad, order = pl.pallas_call(
        grad_kernel,
        grid=(steps,),
        in_specs=[
            pl.BlockSpec(memory_space=pl.ANY),
            pl.BlockSpec(arrived.shape, lambda i: (0, 0, 0)),
            pl.BlockSpec((rows_total, block), lambda i: (0, i)),
            pl.BlockSpec((rows_total, block), lambda i: (0, i)),
        ],
        out_specs=(
            pl.BlockSpec((block, features), lambda i: (i, 0)),
            pl.BlockSpec((8, 128), lambda i: (0, 0)),
        ),
        out_shape=(
            jax.ShapeDtypeStruct((hidden_units, features), jnp.bfloat16),
            jax.ShapeDtypeStruct((8, 128), jnp.float32),
        ),
        scratch_shapes=[
            pltpu.VMEM((rows_total, features), jnp.bfloat16),
            pltpu.VMEM((rows_total, 128), jnp.float32),
        ],
        compiler_params=pltpu.CompilerParams(vmem_limit_bytes=24 << 20),
        name="down_grad",
    )(dots, arrived, hidden, twin_hidden)
    route_part = pl.pallas_call(
        pick_kernel,
        in_specs=[pl.BlockSpec(memory_space=pltpu.VMEM)] * 3 + [pl.BlockSpec(memory_space=pl.ANY)],
        out_shape=jax.ShapeDtypeStruct((top_count, token_count), jnp.float32),
        compiler_params=pltpu.CompilerParams(vmem_limit_bytes=4 << 20),
        name="pick",
    )(returned.reshape(slot_count, pair_rows), target, weight_t, order)
    return (down_grad[None], lax.psum(route_part, "rep").T)


def solution(mesh):
    ep, rep = mesh.shape["ep"], mesh.shape["rep"]
    halves = Mesh(mesh.devices.reshape(2, ep // 2, rep), ("half", "place", "rep"))
    ep = ("half", "place")
    placed = (
        P(ep, "rep"),
        P(ep, None),
        P(ep, None),
        P(),
        P(ep, None),
        P(ep, None, None, "rep"),
        P(ep, None, "rep"),
    )
    return jax.shard_map(
        on_device,
        mesh=halves,
        in_specs=placed,
        out_specs=(P(ep, None, "rep"), P(ep, None)),
        check_vma=False,
    )
```

```python
import functools

import jax
import jax.numpy as jnp
from jax import lax
from jax.experimental import pallas as pl
from jax.experimental.pallas import tpu as pltpu
from jax.sharding import Mesh, PartitionSpec as P


def pack_kernel(ids_ref, weight_ref, slot_expert_ref, pick_ref, grad_ref, rows_ref, target_ref):
    top, tokens = ids_ref.shape
    experts = pick_ref.shape[1]
    slots, pair_rows, _ = rows_ref.shape
    features = grad_ref.shape[1]
    slot_expert = slot_expert_ref[...]
    lane = lax.broadcasted_iota(jnp.int32, (1, slots), 1)
    twin = pltpu.roll(slot_expert, slots // 2, 1)
    shared = jnp.where(twin == slot_expert, 1, 0)
    rank = jnp.where((lane >= slots // 2) & (shared > 0), 1.0, 0.0)
    holds = lax.broadcasted_iota(jnp.int32, (experts, slots), 0) == slot_expert
    pick = jnp.dot(
        pick_ref[...].astype(jnp.bfloat16),
        jnp.where(holds, 1.0, 0.0).astype(jnp.bfloat16),
        preferred_element_type=jnp.float32,
    )
    picked = pick == rank
    serves = holds & picked
    slot_of = jnp.sum(jnp.where(serves, lane, 0).astype(jnp.float32), axis=1, keepdims=True)
    other = jnp.where(shared > 0, jnp.where(lane < slots // 2, slots // 2, -(slots // 2)), 0)
    twin_of = slot_of + jnp.sum(
        jnp.where(serves, other, 0).astype(jnp.float32), axis=1, keepdims=True
    )
    expert = lax.broadcasted_iota(jnp.int32, (experts, tokens), 0)
    chosen = [expert == ids_ref[k : k + 1, :] for k in range(top)]
    named = sum(jnp.where(c, 1.0, 0.0) for c in chosen)
    earlier = lax.broadcasted_iota(jnp.int32, (tokens, tokens), 0) < lax.broadcasted_iota(
        jnp.int32, (tokens, tokens), 1
    )
    before = jnp.dot(
        named.astype(jnp.bfloat16),
        jnp.where(earlier, 1.0, 0.0).astype(jnp.bfloat16),
        preferred_element_type=jnp.float32,
    )
    place = slot_of * pair_rows + before
    twin_place = twin_of * pair_rows + before
    row = lax.broadcasted_iota(jnp.int32, (slots * pair_rows, tokens), 0)
    mix = jnp.zeros((slots * pair_rows, tokens), jnp.float32)
    for k in range(top):
        target = jnp.sum(jnp.where(chosen[k], place, 0.0), axis=0, keepdims=True).astype(jnp.int32)
        twin_target = jnp.sum(jnp.where(chosen[k], twin_place, 0.0), axis=0, keepdims=True)
        target_ref[k : k + 1, :] = target
        here = (row == target) | (row == twin_target.astype(jnp.int32))
        mix += jnp.where(here, weight_ref[k : k + 1, :], 0.0)
    rows = jnp.dot(mix.astype(jnp.bfloat16), grad_ref[...], preferred_element_type=jnp.float32)
    rows_ref[:, :, :features] = rows.astype(rows_ref.dtype).reshape(slots, pair_rows, features)
    slot = lax.broadcasted_iota(jnp.int32, (slots * pair_rows, slots), 0) // pair_rows
    chosen_slot = (slot == lane) & picked
    rows_ref[:, :, features:] = (
        jnp.where(chosen_slot, 1.0, 0.0).astype(rows_ref.dtype).reshape(slots, pair_rows, slots)
    )


def hidden_kernel(saved_ref, out_ref):
    gate = saved_ref[:, 0, :].astype(jnp.float32)
    up = saved_ref[:, 1, :].astype(jnp.float32)
    out_ref[...] = (gate / (1.0 + jnp.exp(-gate)) * up).astype(out_ref.dtype)


def forward_kernel(hidden_ref, weight_ref, out_ref):
    out_ref[...] = jnp.dot(hidden_ref[...], weight_ref[...], preferred_element_type=jnp.float32)


def dots_kernel(arrived_ref, outputs_ref, dots_ref, scratch):
    rows = arrived_ref[:, :, : outputs_ref.shape[1]].reshape(outputs_ref.shape)
    total = jnp.sum(rows.astype(jnp.float32) * outputs_ref[...], axis=1, keepdims=True)
    scratch[...] = jnp.broadcast_to(total, scratch.shape)
    depth = dots_ref.shape[0]
    run = scratch.shape[0] // (2 * depth)
    lane = lax.broadcasted_iota(jnp.int32, dots_ref.shape, 1)
    found = jnp.zeros(dots_ref.shape, jnp.float32)
    for half in range(2):
        for step in range(run):
            part = scratch[pl.ds(half * depth * run + step, depth, stride=run), :]
            found = jnp.where(lane == half * run + step, part, found)
    dots_ref[...] = found


def turn_kernel(arrived_ref, _, out_ref, scratch, *, pair_rows, copies):
    depth = arrived_ref.shape[0]
    scratch[...] = jnp.zeros_like(scratch)
    scratch[:depth, :] = arrived_ref[...]
    scratch[...] = scratch[...].T
    count = out_ref.shape[0] // copies
    turned = scratch[pl.ds(0, count, stride=pair_rows), :]
    for p in range(1, pair_rows):
        turned += pltpu.roll(scratch[pl.ds(p, count, stride=pair_rows), :], p * depth, 1)
    for copy in range(copies):
        out_ref[pl.ds(copy, count, stride=copies), :] = turned


def pick_kernel(returned_ref, target_ref, weight_ref, _, out_ref, scratch, *, depth, width, copies):
    top, tokens = target_ref.shape
    count = returned_ref.shape[0] // copies
    pair_rows = 2
    scratch[...] = jnp.zeros_like(scratch)
    scratch[:count, :] = sum(
        returned_ref[pl.ds(copy, count, stride=copies), :] for copy in range(copies)
    )
    returned = scratch[...].T[: pair_rows * depth, :]
    row = lax.broadcasted_iota(jnp.int32, (pair_rows * depth, tokens), 0)
    for k in range(top):
        target = target_ref[k : k + 1, :]
        slot = target // pair_rows
        place = (target % pair_rows) * depth + slot // width % depth
        column = slot // (width * depth) * width + slot % width
        found = jnp.zeros(row.shape, jnp.float32)
        for c in range(count):
            found += jnp.where((row == place) & (column == c), returned[:, c : c + 1], 0.0)
        weight = weight_ref[k : k + 1, :].astype(jnp.bfloat16).astype(jnp.float32)
        out_ref[k : k + 1, :] = jnp.sum(found, axis=0, keepdims=True) / weight


def grad_kernel(_, arrived_ref, hidden_ref, twin_hidden_ref, out_ref, order_ref, rows_ref, own_ref):
    features = out_ref.shape[1]
    rows = rows_ref.shape[0]

    @pl.when(pl.program_id(0) == 0)
    def _():
        rows_ref[...] = arrived_ref[:, :, :features].reshape(rows_ref.shape)
        picked = arrived_ref[:, :, features:].reshape(rows, arrived_ref.shape[2] - features)
        picked = jnp.sum(picked.astype(jnp.float32), axis=1, keepdims=True)
        own_ref[...] = jnp.broadcast_to(picked, own_ref.shape)
        order_ref[...] = jnp.zeros_like(order_ref)

    own = own_ref[:, :1] > 0.5
    hidden = jnp.where(own, hidden_ref[...], twin_hidden_ref[...])
    out_ref[...] = lax.dot_general(
        hidden, rows_ref[...], (((0,), (0,)), ((), ())), preferred_element_type=jnp.float32
    ).astype(out_ref.dtype)


def on_device(out_grad, route_weight, expert_ids, slot_expert, replica_pick, saved_gu, down_weight):
    ep = ("half", "z", "x")
    sources = lax.axis_size(ep)
    depth, width, copies = lax.axis_size("z"), lax.axis_size("x"), lax.axis_size("rep")
    token_count, top_count = expert_ids.shape
    slot_count = slot_expert.shape[0]
    rows_total = saved_gu.shape[1]
    pair_rows = rows_total // sources
    features = out_grad.shape[1]
    hidden_units = down_weight.shape[1]
    ids_t = expert_ids.T
    weight_t = route_weight.T
    send_rows, target = pl.pallas_call(
        pack_kernel,
        out_shape=(
            jax.ShapeDtypeStruct((slot_count, pair_rows, features + slot_count), jnp.bfloat16),
            jax.ShapeDtypeStruct((top_count, token_count), jnp.int32),
        ),
        name="pack",
    )(ids_t, weight_t, slot_expert[None], replica_pick, out_grad)
    arrived = lax.all_to_all(send_rows, ep, split_axis=0, concat_axis=0, tiled=True)
    part = pl.pallas_call(
        hidden_kernel,
        out_shape=jax.ShapeDtypeStruct((rows_total, saved_gu.shape[3]), jnp.bfloat16),
        compiler_params=pltpu.CompilerParams(vmem_limit_bytes=8 << 20),
        name="hidden",
    )(saved_gu[0])
    twin_part = lax.ppermute(part, "half", [(0, 1), (1, 0)])
    hidden = lax.all_gather(part, "rep", axis=1, tiled=True)
    twin_hidden = lax.all_gather(twin_part, "rep", axis=1, tiled=True)
    outputs = pl.pallas_call(
        forward_kernel,
        out_shape=pltpu.VMEM((rows_total, features), jnp.float32),
        compiler_params=pltpu.CompilerParams(vmem_limit_bytes=12 << 20),
        name="forward",
    )(hidden, down_weight[0])
    dots = pl.pallas_call(
        dots_kernel,
        in_specs=[pl.BlockSpec(memory_space=pltpu.VMEM)] * 2,
        out_shape=jax.ShapeDtypeStruct((depth, 128), jnp.float32),
        scratch_shapes=[pltpu.VMEM((rows_total, 128), jnp.float32)],
        compiler_params=pltpu.CompilerParams(vmem_limit_bytes=8 << 20),
        name="dots",
    )(arrived, outputs)
    along_z = lax.all_to_all(
        dots.reshape(depth, 1, 128), "z", split_axis=0, concat_axis=0, tiled=True
    )
    group = 2 * width * copies
    turned = pl.pallas_call(
        functools.partial(turn_kernel, pair_rows=pair_rows, copies=copies),
        in_specs=[pl.BlockSpec(memory_space=pltpu.VMEM), pl.BlockSpec(memory_space=pl.ANY)],
        out_shape=jax.ShapeDtypeStruct((group, 128), jnp.float32),
        scratch_shapes=[pltpu.VMEM((128, 128), jnp.float32)],
        compiler_params=pltpu.CompilerParams(vmem_limit_bytes=4 << 20),
        name="turn",
    )(along_z.reshape(depth, 128), twin_hidden)
    returned = lax.all_to_all(
        turned.reshape(group, 1, 128),
        ("half", "x", "rep"),
        split_axis=0,
        concat_axis=0,
        tiled=True,
    )
    steps = 2
    block = hidden_units // steps
    down_grad, order = pl.pallas_call(
        grad_kernel,
        grid=(steps,),
        in_specs=[
            pl.BlockSpec(memory_space=pl.ANY),
            pl.BlockSpec(arrived.shape, lambda i: (0, 0, 0)),
            pl.BlockSpec((rows_total, block), lambda i: (0, i)),
            pl.BlockSpec((rows_total, block), lambda i: (0, i)),
        ],
        out_specs=(
            pl.BlockSpec((block, features), lambda i: (i, 0)),
            pl.BlockSpec((8, 128), lambda i: (0, 0)),
        ),
        out_shape=(
            jax.ShapeDtypeStruct((hidden_units, features), jnp.bfloat16),
            jax.ShapeDtypeStruct((8, 128), jnp.float32),
        ),
        scratch_shapes=[
            pltpu.VMEM((rows_total, features), jnp.bfloat16),
            pltpu.VMEM((rows_total, 128), jnp.float32),
        ],
        compiler_params=pltpu.CompilerParams(vmem_limit_bytes=24 << 20),
        name="down_grad",
    )(dots, arrived, hidden, twin_hidden)
    route_grad = pl.pallas_call(
        functools.partial(pick_kernel, depth=depth, width=width, copies=copies),
        in_specs=[pl.BlockSpec(memory_space=pltpu.VMEM)] * 3 + [pl.BlockSpec(memory_space=pl.ANY)],
        out_shape=jax.ShapeDtypeStruct((top_count, token_count), jnp.float32),
        scratch_shapes=[pltpu.VMEM((128, 128), jnp.float32)],
        compiler_params=pltpu.CompilerParams(vmem_limit_bytes=4 << 20),
        name="pick",
    )(returned.reshape(group, 128), target, weight_t, order)
    return (down_grad[None], route_grad.T)


def solution(mesh):
    ep, rep = mesh.shape["ep"], mesh.shape["rep"]
    width = 4
    finer = Mesh(
        mesh.devices.reshape(2, ep // (2 * width), width, rep), ("half", "z", "x", "rep")
    )
    ep = ("half", "z", "x")
    placed = (
        P(ep, "rep"),
        P(ep, None),
        P(ep, None),
        P(),
        P(ep, None),
        P(ep, None, None, "rep"),
        P(ep, None, "rep"),
    )
    return jax.shard_map(
        on_device,
        mesh=finer,
        in_specs=placed,
        out_specs=(P(ep, None, "rep"), P(ep, None)),
        check_vma=False,
    )
```

```python
import functools

import jax
import jax.numpy as jnp
from jax import lax
from jax.experimental import pallas as pl
from jax.experimental.pallas import tpu as pltpu
from jax.sharding import Mesh, PartitionSpec as P


def pack_kernel(ids_ref, weight_ref, slot_expert_ref, pick_ref, grad_ref, rows_ref, target_ref):
    top, tokens = ids_ref.shape
    experts = pick_ref.shape[1]
    slots, pair_rows, _ = rows_ref.shape
    slot_expert = slot_expert_ref[...]
    lane = lax.broadcasted_iota(jnp.int32, (1, slots), 1)
    twin = pltpu.roll(slot_expert, slots // 2, 1)
    shared = jnp.where(twin == slot_expert, 1, 0)
    rank = jnp.where((lane >= slots // 2) & (shared > 0), 1.0, 0.0)
    holds = lax.broadcasted_iota(jnp.int32, (experts, slots), 0) == slot_expert
    pick = jnp.dot(
        pick_ref[...].astype(jnp.bfloat16),
        jnp.where(holds, 1.0, 0.0).astype(jnp.bfloat16),
        preferred_element_type=jnp.float32,
    )
    picked = pick == rank
    serves = holds & picked
    slot_of = jnp.sum(jnp.where(serves, lane, 0).astype(jnp.float32), axis=1, keepdims=True)
    other = jnp.where(shared > 0, jnp.where(lane < slots // 2, slots // 2, -(slots // 2)), 0)
    twin_of = slot_of + jnp.sum(
        jnp.where(serves, other, 0).astype(jnp.float32), axis=1, keepdims=True
    )
    expert = lax.broadcasted_iota(jnp.int32, (experts, tokens), 0)
    chosen = [expert == ids_ref[k : k + 1, :] for k in range(top)]
    named = sum(jnp.where(c, 1.0, 0.0) for c in chosen)
    earlier = lax.broadcasted_iota(jnp.int32, (tokens, tokens), 0) < lax.broadcasted_iota(
        jnp.int32, (tokens, tokens), 1
    )
    before = jnp.dot(
        named.astype(jnp.bfloat16),
        jnp.where(earlier, 1.0, 0.0).astype(jnp.bfloat16),
        preferred_element_type=jnp.float32,
    )
    place = slot_of * pair_rows + before
    twin_place = twin_of * pair_rows + before
    row = lax.broadcasted_iota(jnp.int32, (slots * pair_rows, tokens), 0)
    mix = jnp.zeros((slots * pair_rows, tokens), jnp.float32)
    for k in range(top):
        target = jnp.sum(jnp.where(chosen[k], place, 0.0), axis=0, keepdims=True).astype(jnp.int32)
        twin_target = jnp.sum(jnp.where(chosen[k], twin_place, 0.0), axis=0, keepdims=True)
        target_ref[k : k + 1, :] = target
        here = (row == target) | (row == twin_target.astype(jnp.int32))
        mix += jnp.where(here, weight_ref[k : k + 1, :], 0.0)
    rows = jnp.dot(mix.astype(jnp.bfloat16), grad_ref[...], preferred_element_type=jnp.float32)
    rows_ref[...] = rows.astype(rows_ref.dtype).reshape(rows_ref.shape)


def hidden_kernel(saved_ref, pick_ref, out_ref, bundle_ref):
    gate = saved_ref[:, 0, :].astype(jnp.float32)
    up = saved_ref[:, 1, :].astype(jnp.float32)
    hidden = (gate / (1.0 + jnp.exp(-gate)) * up).astype(out_ref.dtype)
    out_ref[...] = hidden
    rows, experts = out_ref.shape[0], pick_ref.shape[1]
    bundle_ref[:rows, :] = hidden
    below = bundle_ref.shape[0] - rows
    bundle_ref[rows:, :] = jnp.zeros((below, out_ref.shape[1]), out_ref.dtype)
    pick = pick_ref[...].astype(jnp.float32).astype(out_ref.dtype)
    bundle_ref[rows:, :experts] = jnp.broadcast_to(pick, (below, experts))


def mark_kernel(pick_ref, twin_ref, slot_expert_ref, out_ref, scratch, *, first):
    experts = pick_ref.shape[1]
    slots = slot_expert_ref.shape[1]
    slot_expert = slot_expert_ref[...]
    lane = lax.broadcasted_iota(jnp.int32, (1, slots), 1)
    twin = pltpu.roll(slot_expert, slots // 2, 1)
    rank = jnp.where((lane >= slots // 2) & (twin == slot_expert), 1.0, 0.0)
    holds = lax.broadcasted_iota(jnp.int32, (experts, slots), 0) == slot_expert
    holds = jnp.where(holds, 1.0, 0.0).astype(jnp.bfloat16)
    half = lax.axis_index("half")
    own = jnp.dot(pick_ref[...].astype(jnp.bfloat16), holds, preferred_element_type=jnp.float32)
    other = twin_ref[twin_ref.shape[0] - 16 :, :experts]
    other = jnp.dot(other, holds, preferred_element_type=jnp.float32)[:1, :]
    scratch[...] = jnp.zeros_like(scratch)
    for source in range(2):
        pick = jnp.where(half == source, own, other)
        scratch[source : source + 1, :] = jnp.where(pick == rank, 1.0, 0.0)
    scratch[...] = scratch[...].T
    places = out_ref.shape[0]
    held = scratch[pl.ds(pl.multiple_of(half * places, places), places), :]
    out_ref[...] = pltpu.roll(held, first, 1)


def forward_kernel(hidden_ref, weight_ref, out_ref):
    out_ref[...] = jnp.dot(hidden_ref[...], weight_ref[...], preferred_element_type=jnp.float32)


def dots_kernel(arrived_ref, outputs_ref, marks_ref, dots_ref, scratch):
    rows = arrived_ref[...].reshape(outputs_ref.shape)
    total = jnp.sum(rows.astype(jnp.float32) * outputs_ref[...], axis=1, keepdims=True)
    scratch[...] = jnp.broadcast_to(total, scratch.shape)
    places = dots_ref.shape[0]
    pair_rows = arrived_ref.shape[1]
    lane = lax.broadcasted_iota(jnp.int32, dots_ref.shape, 1)
    found = marks_ref[...]
    for half in range(2):
        for p in range(pair_rows):
            part = scratch[pl.ds(half * places * pair_rows + p, places, stride=pair_rows), :]
            found = jnp.where(lane == half * pair_rows + p, part, found)
    dots_ref[...] = found


def turn_kernel(arrived_ref, _, out_ref, scratch, *, pair_rows, copies):
    places = arrived_ref.shape[0]
    scratch[...] = jnp.zeros_like(scratch)
    scratch[:places, :] = arrived_ref[...]
    turned = scratch[...].T
    for half in range(2):
        row = turned[half * pair_rows : half * pair_rows + 1, :]
        for p in range(1, pair_rows):
            other = turned[half * pair_rows + p : half * pair_rows + p + 1, :]
            row += pltpu.roll(other, p * places, 1)
        out_ref[half * copies : (half + 1) * copies, :] = jnp.broadcast_to(
            row, (copies, out_ref.shape[1])
        )


def pick_kernel(returned_ref, target_ref, weight_ref, _, out_ref, scratch, *, places, copies):
    top, tokens = target_ref.shape
    pair_rows = 2
    scratch[...] = jnp.zeros_like(scratch)
    for half in range(2):
        scratch[half : half + 1, :] = jnp.sum(
            returned_ref[half * copies : (half + 1) * copies, :], axis=0, keepdims=True
        )
    returned = scratch[...].T
    row = lax.broadcasted_iota(jnp.int32, (returned.shape[0], tokens), 0)
    for k in range(top):
        target = target_ref[k : k + 1, :]
        slot = target // pair_rows
        here = row == (target % pair_rows) * places + slot % places
        found = jnp.where(here, jnp.where(slot < places, returned[:, :1], returned[:, 1:2]), 0.0)
        weight = weight_ref[k : k + 1, :].astype(jnp.bfloat16).astype(jnp.float32)
        out_ref[k : k + 1, :] = jnp.sum(found, axis=0, keepdims=True) / weight


def grad_kernel(
    _, arrived_ref, marks_ref, hidden_ref, twin_hidden_ref, out_ref, order_ref, rows_ref, own_ref, *, first
):
    places = marks_ref.shape[0]
    pair_rows = arrived_ref.shape[1]

    @pl.when(pl.program_id(0) == 0)
    def _():
        rows_ref[...] = arrived_ref[...].reshape(rows_ref.shape)
        for half in range(2):
            mark = jnp.broadcast_to(
                marks_ref[:, first + half : first + half + 1], (places, own_ref.shape[1])
            )
            for p in range(pair_rows):
                own_ref[pl.ds(half * places * pair_rows + p, places, stride=pair_rows), :] = mark
        order_ref[...] = jnp.zeros_like(order_ref)

    own = own_ref[:, :1] > 0.5
    hidden = jnp.where(own, hidden_ref[...], twin_hidden_ref[...])
    out_ref[...] = lax.dot_general(
        hidden, rows_ref[...], (((0,), (0,)), ((), ())), preferred_element_type=jnp.float32
    ).astype(out_ref.dtype)


def on_device(out_grad, route_weight, expert_ids, slot_expert, replica_pick, saved_gu, down_weight):
    ep = ("half", "place")
    sources = lax.axis_size(ep)
    places, copies = lax.axis_size("place"), lax.axis_size("rep")
    token_count, top_count = expert_ids.shape
    slot_count = slot_expert.shape[0]
    rows_total = saved_gu.shape[1]
    pair_rows = rows_total // sources
    features = out_grad.shape[1]
    hidden_units = down_weight.shape[1]
    ids_t = expert_ids.T
    weight_t = route_weight.T
    send_rows, target = pl.pallas_call(
        pack_kernel,
        out_shape=(
            jax.ShapeDtypeStruct((slot_count, pair_rows, features), jnp.bfloat16),
            jax.ShapeDtypeStruct((top_count, token_count), jnp.int32),
        ),
        name="pack",
    )(ids_t, weight_t, slot_expert[None], replica_pick, out_grad)
    arrived = lax.all_to_all(send_rows, ep, split_axis=0, concat_axis=0, tiled=True)
    marked = 2 * pair_rows
    units = saved_gu.shape[3]
    part, bundle = pl.pallas_call(
        hidden_kernel,
        out_shape=(
            jax.ShapeDtypeStruct((rows_total, units), jnp.bfloat16),
            jax.ShapeDtypeStruct((rows_total + 16, units), jnp.bfloat16),
        ),
        compiler_params=pltpu.CompilerParams(vmem_limit_bytes=8 << 20),
        name="hidden",
    )(saved_gu[0], replica_pick)
    bundle = lax.ppermute(bundle, "half", [(0, 1), (1, 0)])
    marks = pl.pallas_call(
        functools.partial(mark_kernel, first=marked),
        in_specs=[pl.BlockSpec(memory_space=pltpu.VMEM)] * 3,
        out_shape=jax.ShapeDtypeStruct((places, slot_count), jnp.float32),
        scratch_shapes=[pltpu.VMEM((slot_count, slot_count), jnp.float32)],
        compiler_params=pltpu.CompilerParams(vmem_limit_bytes=4 << 20),
        name="marks",
    )(replica_pick, bundle, slot_expert[None])
    hidden = lax.all_gather(part, "rep", axis=1, tiled=True)
    twin_hidden = lax.all_gather(bundle, "rep", axis=1, tiled=True)
    outputs = pl.pallas_call(
        forward_kernel,
        out_shape=pltpu.VMEM((rows_total, features), jnp.float32),
        compiler_params=pltpu.CompilerParams(vmem_limit_bytes=12 << 20),
        name="forward",
    )(hidden, down_weight[0])
    dots = pl.pallas_call(
        dots_kernel,
        in_specs=[pl.BlockSpec(memory_space=pltpu.VMEM)] * 3,
        out_shape=jax.ShapeDtypeStruct((places, 128), jnp.float32),
        scratch_shapes=[pltpu.VMEM((rows_total, 128), jnp.float32)],
        compiler_params=pltpu.CompilerParams(vmem_limit_bytes=8 << 20),
        name="dots",
    )(arrived, outputs, marks)
    met = lax.all_to_all(
        dots.reshape(places, 1, 128), "place", split_axis=0, concat_axis=0, tiled=True
    ).reshape(places, 128)
    group = 2 * copies
    turned = pl.pallas_call(
        functools.partial(turn_kernel, pair_rows=pair_rows, copies=copies),
        in_specs=[pl.BlockSpec(memory_space=pltpu.VMEM), pl.BlockSpec(memory_space=pl.ANY)],
        out_shape=jax.ShapeDtypeStruct((group, 128), jnp.float32),
        scratch_shapes=[pltpu.VMEM((128, 128), jnp.float32)],
        compiler_params=pltpu.CompilerParams(vmem_limit_bytes=4 << 20),
        name="turn",
    )(met, twin_hidden)
    returned = lax.all_to_all(
        turned.reshape(group, 1, 128),
        ("half", "rep"),
        split_axis=0,
        concat_axis=0,
        tiled=True,
    )
    steps = 2
    block = hidden_units // steps
    down_grad, order = pl.pallas_call(
        functools.partial(grad_kernel, first=marked),
        grid=(steps,),
        in_specs=[
            pl.BlockSpec(memory_space=pl.ANY),
            pl.BlockSpec(arrived.shape, lambda i: (0, 0, 0)),
            pl.BlockSpec((places, 128), lambda i: (0, 0)),
            pl.BlockSpec((rows_total, block), lambda i: (0, i)),
            pl.BlockSpec((rows_total, block), lambda i: (0, i)),
        ],
        out_specs=(
            pl.BlockSpec((block, features), lambda i: (i, 0)),
            pl.BlockSpec((8, 128), lambda i: (0, 0)),
        ),
        out_shape=(
            jax.ShapeDtypeStruct((hidden_units, features), jnp.bfloat16),
            jax.ShapeDtypeStruct((8, 128), jnp.float32),
        ),
        scratch_shapes=[
            pltpu.VMEM((rows_total, features), jnp.bfloat16),
            pltpu.VMEM((rows_total, 128), jnp.float32),
        ],
        compiler_params=pltpu.CompilerParams(vmem_limit_bytes=24 << 20),
        name="down_grad",
    )(turned, arrived, met, hidden, twin_hidden)
    route_grad = pl.pallas_call(
        functools.partial(pick_kernel, places=places, copies=copies),
        in_specs=[pl.BlockSpec(memory_space=pltpu.VMEM)] * 3 + [pl.BlockSpec(memory_space=pl.ANY)],
        out_shape=jax.ShapeDtypeStruct((top_count, token_count), jnp.float32),
        scratch_shapes=[pltpu.VMEM((128, 128), jnp.float32)],
        compiler_params=pltpu.CompilerParams(vmem_limit_bytes=4 << 20),
        name="pick",
    )(returned.reshape(group, 128), target, weight_t, order)
    return (down_grad[None], route_grad.T)


def solution(mesh):
    ep, rep = mesh.shape["ep"], mesh.shape["rep"]
    halves = Mesh(mesh.devices.reshape(2, ep // 2, rep), ("half", "place", "rep"))
    ep = ("half", "place")
    placed = (
        P(ep, "rep"),
        P(ep, None),
        P(ep, None),
        P(),
        P(ep, None),
        P(ep, None, None, "rep"),
        P(ep, None, "rep"),
    )
    return jax.shard_map(
        on_device,
        mesh=halves,
        in_specs=placed,
        out_specs=(P(ep, None, "rep"), P(ep, None)),
        check_vma=False,
    )
```

```python
import functools

import jax
import jax.numpy as jnp
from jax import lax
from jax.experimental import pallas as pl
from jax.experimental.pallas import tpu as pltpu
from jax.sharding import Mesh, PartitionSpec as P


def pack_kernel(ids_ref, weight_ref, slot_expert_ref, pick_ref, grad_ref, rows_ref, target_ref):
    top, tokens = ids_ref.shape
    experts = pick_ref.shape[1]
    slots, pair_rows, _ = rows_ref.shape
    slot_expert = slot_expert_ref[...]
    lane = lax.broadcasted_iota(jnp.int32, (1, slots), 1)
    twin = pltpu.roll(slot_expert, slots // 2, 1)
    shared = jnp.where(twin == slot_expert, 1, 0)
    rank = jnp.where((lane >= slots // 2) & (shared > 0), 1.0, 0.0)
    holds = lax.broadcasted_iota(jnp.int32, (experts, slots), 0) == slot_expert
    pick = jnp.dot(
        pick_ref[...].astype(jnp.bfloat16),
        jnp.where(holds, 1.0, 0.0).astype(jnp.bfloat16),
        preferred_element_type=jnp.float32,
    )
    picked = pick == rank
    serves = holds & picked
    slot_of = jnp.sum(jnp.where(serves, lane, 0).astype(jnp.float32), axis=1, keepdims=True)
    other = jnp.where(shared > 0, jnp.where(lane < slots // 2, slots // 2, -(slots // 2)), 0)
    twin_of = slot_of + jnp.sum(
        jnp.where(serves, other, 0).astype(jnp.float32), axis=1, keepdims=True
    )
    expert = lax.broadcasted_iota(jnp.int32, (experts, tokens), 0)
    chosen = [expert == ids_ref[k : k + 1, :] for k in range(top)]
    named = sum(jnp.where(c, 1.0, 0.0) for c in chosen)
    earlier = lax.broadcasted_iota(jnp.int32, (tokens, tokens), 0) < lax.broadcasted_iota(
        jnp.int32, (tokens, tokens), 1
    )
    before = jnp.dot(
        named.astype(jnp.bfloat16),
        jnp.where(earlier, 1.0, 0.0).astype(jnp.bfloat16),
        preferred_element_type=jnp.float32,
    )
    place = slot_of * pair_rows + before
    twin_place = twin_of * pair_rows + before
    row = lax.broadcasted_iota(jnp.int32, (slots * pair_rows, tokens), 0) ^ (slots // 4 * pair_rows)
    mix = jnp.zeros((slots * pair_rows, tokens), jnp.float32)
    for k in range(top):
        target = jnp.sum(jnp.where(chosen[k], place, 0.0), axis=0, keepdims=True).astype(jnp.int32)
        twin_target = jnp.sum(jnp.where(chosen[k], twin_place, 0.0), axis=0, keepdims=True)
        target_ref[k : k + 1, :] = target
        here = (row == target) | (row == twin_target.astype(jnp.int32))
        mix += jnp.where(here, weight_ref[k : k + 1, :], 0.0)
    rows = jnp.dot(mix.astype(jnp.bfloat16), grad_ref[...], preferred_element_type=jnp.float32)
    rows_ref[...] = rows.astype(rows_ref.dtype).reshape(rows_ref.shape)


def in_place(ref, start, count):
    middle = count // 2
    return [ref[start + middle : start + count], ref[start : start + middle]]


def hidden_kernel(saved_ref, pick_ref, out_ref, bundle_ref):
    gate = saved_ref[:, 0, :].astype(jnp.float32)
    up = saved_ref[:, 1, :].astype(jnp.float32)
    hidden = (gate / (1.0 + jnp.exp(-gate)) * up).astype(out_ref.dtype)
    out_ref[...] = hidden
    rows, experts = out_ref.shape[0], pick_ref.shape[1]
    bundle_ref[:rows, :] = hidden
    below = bundle_ref.shape[0] - rows
    bundle_ref[rows:, :] = jnp.zeros((below, out_ref.shape[1]), out_ref.dtype)
    pick = pick_ref[...].astype(jnp.float32).astype(out_ref.dtype)
    bundle_ref[rows:, :experts] = jnp.broadcast_to(pick, (below, experts))


def mark_kernel(pick_ref, twin_ref, slot_expert_ref, out_ref, scratch, *, first):
    experts = pick_ref.shape[1]
    slots = slot_expert_ref.shape[1]
    slot_expert = slot_expert_ref[...]
    lane = lax.broadcasted_iota(jnp.int32, (1, slots), 1)
    twin = pltpu.roll(slot_expert, slots // 2, 1)
    rank = jnp.where((lane >= slots // 2) & (twin == slot_expert), 1.0, 0.0)
    holds = lax.broadcasted_iota(jnp.int32, (experts, slots), 0) == slot_expert
    holds = jnp.where(holds, 1.0, 0.0).astype(jnp.bfloat16)
    half = lax.axis_index("half")
    own = jnp.dot(pick_ref[...].astype(jnp.bfloat16), holds, preferred_element_type=jnp.float32)
    other = twin_ref[twin_ref.shape[0] - 16 :, :experts]
    other = jnp.dot(other, holds, preferred_element_type=jnp.float32)[:1, :]
    scratch[...] = jnp.zeros_like(scratch)
    for source in range(2):
        pick = jnp.where(half == source, own, other)
        scratch[source : source + 1, :] = jnp.where(pick == rank, 1.0, 0.0)
    scratch[...] = scratch[...].T
    places = out_ref.shape[0]
    held = scratch[pl.ds(pl.multiple_of(half * places, places), places), :]
    out_ref[...] = pltpu.roll(held, first, 1)


def forward_kernel(hidden_ref, weight_ref, out_ref):
    out_ref[...] = jnp.dot(hidden_ref[...], weight_ref[...], preferred_element_type=jnp.float32)


def dots_kernel(arrived_ref, outputs_ref, marks_ref, dots_ref, scratch):
    places = dots_ref.shape[0]
    pair_rows, features = arrived_ref.shape[1:]
    size = places // 2 * pair_rows
    blocks = in_place(arrived_ref, 0, places) + in_place(arrived_ref, places, places)
    for number, block in enumerate(blocks):
        here = slice(number * size, (number + 1) * size)
        rows = block.reshape(size, features).astype(jnp.float32)
        total = jnp.sum(rows * outputs_ref[here, :], axis=1, keepdims=True)
        scratch[here, :] = jnp.broadcast_to(total, (size, scratch.shape[1]))
    lane = lax.broadcasted_iota(jnp.int32, dots_ref.shape, 1)
    found = marks_ref[...]
    for half in range(2):
        for p in range(pair_rows):
            part = scratch[pl.ds(half * places * pair_rows + p, places, stride=pair_rows), :]
            found = jnp.where(lane == half * pair_rows + p, part, found)
    dots_ref[: places // 2, :] = found[places // 2 :, :]
    dots_ref[places // 2 :, :] = found[: places // 2, :]


def turn_kernel(arrived_ref, _, out_ref, scratch, *, pair_rows, copies):
    places = arrived_ref.shape[0]
    scratch[...] = jnp.zeros_like(scratch)
    for number, block in enumerate(in_place(arrived_ref, 0, places)):
        scratch[number * places // 2 : (number + 1) * places // 2, :] = block
    turned = scratch[...].T
    for half in range(2):
        row = turned[half * pair_rows : half * pair_rows + 1, :]
        for p in range(1, pair_rows):
            other = turned[half * pair_rows + p : half * pair_rows + p + 1, :]
            row += pltpu.roll(other, p * places, 1)
        out_ref[half * copies : (half + 1) * copies, :] = jnp.broadcast_to(
            row, (copies, out_ref.shape[1])
        )


def pick_kernel(returned_ref, target_ref, weight_ref, _, out_ref, scratch, *, places, copies):
    top, tokens = target_ref.shape
    pair_rows = 2
    scratch[...] = jnp.zeros_like(scratch)
    for half in range(2):
        scratch[half : half + 1, :] = jnp.sum(
            returned_ref[half * copies : (half + 1) * copies, :], axis=0, keepdims=True
        )
    returned = scratch[...].T
    row = lax.broadcasted_iota(jnp.int32, (returned.shape[0], tokens), 0)
    for k in range(top):
        target = target_ref[k : k + 1, :]
        slot = target // pair_rows
        here = row == (target % pair_rows) * places + slot % places
        found = jnp.where(here, jnp.where(slot < places, returned[:, :1], returned[:, 1:2]), 0.0)
        weight = weight_ref[k : k + 1, :].astype(jnp.bfloat16).astype(jnp.float32)
        out_ref[k : k + 1, :] = jnp.sum(found, axis=0, keepdims=True) / weight


def grad_kernel(
    _, arrived_ref, marks_ref, hidden_ref, twin_hidden_ref, out_ref, order_ref, rows_ref, own_ref, *, first
):
    places = marks_ref.shape[0]
    pair_rows = arrived_ref.shape[1]

    @pl.when(pl.program_id(0) == 0)
    def _():
        size = places // 2 * pair_rows
        blocks = in_place(arrived_ref, 0, places) + in_place(arrived_ref, places, places)
        for number, block in enumerate(blocks):
            rows_ref[number * size : (number + 1) * size, :] = block.reshape(size, block.shape[2])
        marks = in_place(marks_ref, 0, places)
        for number in range(4):
            half = number // 2
            mark = jnp.broadcast_to(
                marks[number % 2][:, first + half : first + half + 1], (places // 2, own_ref.shape[1])
            )
            for p in range(pair_rows):
                own_ref[pl.ds(number * size + p, places // 2, stride=pair_rows), :] = mark
        order_ref[...] = jnp.zeros_like(order_ref)

    own = own_ref[:, :1] > 0.5
    hidden = jnp.where(own, hidden_ref[...], twin_hidden_ref[...])
    out_ref[...] = lax.dot_general(
        hidden, rows_ref[...], (((0,), (0,)), ((), ())), preferred_element_type=jnp.float32
    ).astype(out_ref.dtype)


def on_device(out_grad, route_weight, expert_ids, slot_expert, replica_pick, saved_gu, down_weight):
    ep = ("half", "place")
    sources = lax.axis_size(ep)
    places, copies = lax.axis_size("place"), lax.axis_size("rep")
    token_count, top_count = expert_ids.shape
    slot_count = slot_expert.shape[0]
    rows_total = saved_gu.shape[1]
    pair_rows = rows_total // sources
    features = out_grad.shape[1]
    hidden_units = down_weight.shape[1]
    ids_t = expert_ids.T
    weight_t = route_weight.T
    send_rows, target = pl.pallas_call(
        pack_kernel,
        out_shape=(
            jax.ShapeDtypeStruct((slot_count, pair_rows, features), jnp.bfloat16),
            jax.ShapeDtypeStruct((top_count, token_count), jnp.int32),
        ),
        name="pack",
    )(ids_t, weight_t, slot_expert[None], replica_pick, out_grad)
    around = [(i + places // 2) % places for i in range(places)]
    arrived = lax.all_to_all(
        send_rows,
        ep,
        split_axis=0,
        concat_axis=0,
        axis_index_groups=[around + [places + i for i in around]],
        tiled=True,
    )
    marked = 2 * pair_rows
    units = saved_gu.shape[3]
    part, bundle = pl.pallas_call(
        hidden_kernel,
        out_shape=(
            jax.ShapeDtypeStruct((rows_total, units), jnp.bfloat16),
            jax.ShapeDtypeStruct((rows_total + 16, units), jnp.bfloat16),
        ),
        compiler_params=pltpu.CompilerParams(vmem_limit_bytes=8 << 20),
        name="hidden",
    )(saved_gu[0], replica_pick)
    bundle = lax.ppermute(bundle, "half", [(0, 1), (1, 0)])
    marks = pl.pallas_call(
        functools.partial(mark_kernel, first=marked),
        in_specs=[pl.BlockSpec(memory_space=pltpu.VMEM)] * 3,
        out_shape=jax.ShapeDtypeStruct((places, slot_count), jnp.float32),
        scratch_shapes=[pltpu.VMEM((slot_count, slot_count), jnp.float32)],
        compiler_params=pltpu.CompilerParams(vmem_limit_bytes=4 << 20),
        name="marks",
    )(replica_pick, bundle, slot_expert[None])
    hidden = lax.all_gather(part, "rep", axis=1, tiled=True)
    twin_hidden = lax.all_gather(bundle, "rep", axis=1, tiled=True)
    outputs = pl.pallas_call(
        forward_kernel,
        out_shape=pltpu.VMEM((rows_total, features), jnp.float32),
        compiler_params=pltpu.CompilerParams(vmem_limit_bytes=12 << 20),
        name="forward",
    )(hidden, down_weight[0])
    dots = pl.pallas_call(
        dots_kernel,
        in_specs=[pl.BlockSpec(memory_space=pltpu.VMEM)] * 3,
        out_shape=jax.ShapeDtypeStruct((places, 128), jnp.float32),
        scratch_shapes=[pltpu.VMEM((rows_total, 128), jnp.float32)],
        compiler_params=pltpu.CompilerParams(vmem_limit_bytes=8 << 20),
        name="dots",
    )(arrived, outputs, marks)
    met = lax.all_to_all(
        dots.reshape(places, 1, 128),
        "place",
        split_axis=0,
        concat_axis=0,
        axis_index_groups=[around],
        tiled=True,
    ).reshape(places, 128)
    group = 2 * copies
    turned = pl.pallas_call(
        functools.partial(turn_kernel, pair_rows=pair_rows, copies=copies),
        in_specs=[pl.BlockSpec(memory_space=pltpu.VMEM), pl.BlockSpec(memory_space=pl.ANY)],
        out_shape=jax.ShapeDtypeStruct((group, 128), jnp.float32),
        scratch_shapes=[pltpu.VMEM((128, 128), jnp.float32)],
        compiler_params=pltpu.CompilerParams(vmem_limit_bytes=4 << 20),
        name="turn",
    )(met, twin_hidden)
    returned = lax.all_to_all(
        turned.reshape(group, 1, 128),
        ("half", "rep"),
        split_axis=0,
        concat_axis=0,
        tiled=True,
    )
    steps = 2
    block = hidden_units // steps
    down_grad, order = pl.pallas_call(
        functools.partial(grad_kernel, first=marked),
        grid=(steps,),
        in_specs=[
            pl.BlockSpec(memory_space=pl.ANY),
            pl.BlockSpec(arrived.shape, lambda i: (0, 0, 0)),
            pl.BlockSpec((places, 128), lambda i: (0, 0)),
            pl.BlockSpec((rows_total, block), lambda i: (0, i)),
            pl.BlockSpec((rows_total, block), lambda i: (0, i)),
        ],
        out_specs=(
            pl.BlockSpec((block, features), lambda i: (i, 0)),
            pl.BlockSpec((8, 128), lambda i: (0, 0)),
        ),
        out_shape=(
            jax.ShapeDtypeStruct((hidden_units, features), jnp.bfloat16),
            jax.ShapeDtypeStruct((8, 128), jnp.float32),
        ),
        scratch_shapes=[
            pltpu.VMEM((rows_total, features), jnp.bfloat16),
            pltpu.VMEM((rows_total, 128), jnp.float32),
        ],
        compiler_params=pltpu.CompilerParams(vmem_limit_bytes=24 << 20),
        name="down_grad",
    )(turned, arrived, met, hidden, twin_hidden)
    route_grad = pl.pallas_call(
        functools.partial(pick_kernel, places=places, copies=copies),
        in_specs=[pl.BlockSpec(memory_space=pltpu.VMEM)] * 3 + [pl.BlockSpec(memory_space=pl.ANY)],
        out_shape=jax.ShapeDtypeStruct((top_count, token_count), jnp.float32),
        scratch_shapes=[pltpu.VMEM((128, 128), jnp.float32)],
        compiler_params=pltpu.CompilerParams(vmem_limit_bytes=4 << 20),
        name="pick",
    )(returned.reshape(group, 128), target, weight_t, order)
    return (down_grad[None], route_grad.T)


def solution(mesh):
    ep, rep = mesh.shape["ep"], mesh.shape["rep"]
    halves = Mesh(mesh.devices.reshape(2, ep // 2, rep), ("half", "place", "rep"))
    ep = ("half", "place")
    placed = (
        P(ep, "rep"),
        P(ep, None),
        P(ep, None),
        P(),
        P(ep, None),
        P(ep, None, None, "rep"),
        P(ep, None, "rep"),
    )
    return jax.shard_map(
        on_device,
        mesh=halves,
        in_specs=placed,
        out_specs=(P(ep, None, "rep"), P(ep, None)),
        check_vma=False,
    )
```

```python
import functools

import jax
import jax.numpy as jnp
from jax import lax
from jax.experimental import pallas as pl
from jax.experimental.pallas import tpu as pltpu
from jax.sharding import Mesh, PartitionSpec as P


def pack_kernel(ids_ref, weight_ref, slot_expert_ref, pick_ref, grad_ref, rows_ref, target_ref):
    top, tokens = ids_ref.shape
    experts = pick_ref.shape[1]
    slots, pair_rows, _ = rows_ref.shape
    slot_expert = slot_expert_ref[...]
    lane = lax.broadcasted_iota(jnp.int32, (1, slots), 1)
    twin = pltpu.roll(slot_expert, slots // 2, 1)
    shared = jnp.where(twin == slot_expert, 1, 0)
    rank = jnp.where((lane >= slots // 2) & (shared > 0), 1.0, 0.0)
    holds = lax.broadcasted_iota(jnp.int32, (experts, slots), 0) == slot_expert
    pick = jnp.dot(
        pick_ref[...].astype(jnp.bfloat16),
        jnp.where(holds, 1.0, 0.0).astype(jnp.bfloat16),
        preferred_element_type=jnp.float32,
    )
    picked = pick == rank
    serves = holds & picked
    slot_of = jnp.sum(jnp.where(serves, lane, 0).astype(jnp.float32), axis=1, keepdims=True)
    other = jnp.where(shared > 0, jnp.where(lane < slots // 2, slots // 2, -(slots // 2)), 0)
    twin_of = slot_of + jnp.sum(
        jnp.where(serves, other, 0).astype(jnp.float32), axis=1, keepdims=True
    )
    expert = lax.broadcasted_iota(jnp.int32, (experts, tokens), 0)
    chosen = [expert == ids_ref[k : k + 1, :] for k in range(top)]
    named = sum(jnp.where(c, 1.0, 0.0) for c in chosen)
    earlier = lax.broadcasted_iota(jnp.int32, (tokens, tokens), 0) < lax.broadcasted_iota(
        jnp.int32, (tokens, tokens), 1
    )
    before = jnp.dot(
        named.astype(jnp.bfloat16),
        jnp.where(earlier, 1.0, 0.0).astype(jnp.bfloat16),
        preferred_element_type=jnp.float32,
    )
    place = slot_of * pair_rows + before
    twin_place = twin_of * pair_rows + before
    row = lax.broadcasted_iota(jnp.int32, (slots * pair_rows, tokens), 0) ^ (slots // 4 * pair_rows)
    mix = jnp.zeros((slots * pair_rows, tokens), jnp.float32)
    for k in range(top):
        target = jnp.sum(jnp.where(chosen[k], place, 0.0), axis=0, keepdims=True).astype(jnp.int32)
        twin_target = jnp.sum(jnp.where(chosen[k], twin_place, 0.0), axis=0, keepdims=True)
        target_ref[k : k + 1, :] = target
        here = (row == target) | (row == twin_target.astype(jnp.int32))
        mix += jnp.where(here, weight_ref[k : k + 1, :], 0.0)
    rows = jnp.dot(mix.astype(jnp.bfloat16), grad_ref[...], preferred_element_type=jnp.float32)
    rows_ref[...] = rows.astype(rows_ref.dtype).reshape(rows_ref.shape)


def in_place(ref, start, count):
    middle = count // 2
    return [ref[start + middle : start + count], ref[start : start + middle]]


def hidden_kernel(saved_ref, out_ref):
    gate = saved_ref[:, 0, :].astype(jnp.float32)
    up = saved_ref[:, 1, :].astype(jnp.float32)
    out_ref[...] = (gate / (1.0 + jnp.exp(-gate)) * up).astype(out_ref.dtype)


def mark_kernel(pick_ref, twin_ref, slot_expert_ref, out_ref, scratch, *, first):
    experts = pick_ref.shape[1]
    slots = slot_expert_ref.shape[1]
    slot_expert = slot_expert_ref[...]
    lane = lax.broadcasted_iota(jnp.int32, (1, slots), 1)
    twin = pltpu.roll(slot_expert, slots // 2, 1)
    rank = jnp.where((lane >= slots // 2) & (twin == slot_expert), 1.0, 0.0)
    holds = lax.broadcasted_iota(jnp.int32, (experts, slots), 0) == slot_expert
    holds = jnp.where(holds, 1.0, 0.0).astype(jnp.bfloat16)
    half = lax.axis_index("half")
    own, other = (
        jnp.dot(ref[...].astype(jnp.bfloat16), holds, preferred_element_type=jnp.float32)
        for ref in (pick_ref, twin_ref)
    )
    scratch[...] = jnp.zeros_like(scratch)
    for source in range(2):
        pick = jnp.where(half == source, own, other)
        scratch[source : source + 1, :] = jnp.where(pick == rank, 1.0, 0.0)
    scratch[...] = scratch[...].T
    places = out_ref.shape[0]
    held = scratch[pl.ds(pl.multiple_of(half * places, places), places), :]
    out_ref[...] = pltpu.roll(held, first, 1)


def forward_kernel(hidden_ref, weight_ref, out_ref):
    out_ref[...] = jnp.dot(hidden_ref[...], weight_ref[...], preferred_element_type=jnp.float32)


def dots_kernel(arrived_ref, outputs_ref, marks_ref, dots_ref, scratch):
    places = dots_ref.shape[0]
    pair_rows, features = arrived_ref.shape[1:]
    size = places // 2 * pair_rows
    blocks = in_place(arrived_ref, 0, places) + in_place(arrived_ref, places, places)
    for number, block in enumerate(blocks):
        here = slice(number * size, (number + 1) * size)
        rows = block.reshape(size, features).astype(jnp.float32)
        total = jnp.sum(rows * outputs_ref[here, :], axis=1, keepdims=True)
        scratch[here, :] = jnp.broadcast_to(total, (size, scratch.shape[1]))
    lane = lax.broadcasted_iota(jnp.int32, dots_ref.shape, 1)
    found = marks_ref[...]
    for half in range(2):
        for p in range(pair_rows):
            part = scratch[pl.ds(half * places * pair_rows + p, places, stride=pair_rows), :]
            found = jnp.where(lane == half * pair_rows + p, part, found)
    dots_ref[: places // 2, :] = found[places // 2 :, :]
    dots_ref[places // 2 :, :] = found[: places // 2, :]


def turn_kernel(arrived_ref, out_ref, scratch, *, pair_rows, copies):
    places = arrived_ref.shape[0]
    scratch[...] = jnp.zeros_like(scratch)
    for number, block in enumerate(in_place(arrived_ref, 0, places)):
        scratch[number * places // 2 : (number + 1) * places // 2, :] = block
    turned = scratch[...].T
    for half in range(2):
        row = turned[half * pair_rows : half * pair_rows + 1, :]
        for p in range(1, pair_rows):
            other = turned[half * pair_rows + p : half * pair_rows + p + 1, :]
            row += pltpu.roll(other, p * places, 1)
        out_ref[half * copies : (half + 1) * copies, :] = jnp.broadcast_to(
            row, (copies, out_ref.shape[1])
        )


def pick_kernel(returned_ref, target_ref, weight_ref, _, out_ref, scratch, *, places, copies):
    top, tokens = target_ref.shape
    pair_rows = 2
    scratch[...] = jnp.zeros_like(scratch)
    for half in range(2):
        scratch[half : half + 1, :] = jnp.sum(
            returned_ref[half * copies : (half + 1) * copies, :], axis=0, keepdims=True
        )
    returned = scratch[...].T
    row = lax.broadcasted_iota(jnp.int32, (returned.shape[0], tokens), 0)
    for k in range(top):
        target = target_ref[k : k + 1, :]
        slot = target // pair_rows
        here = row == (target % pair_rows) * places + slot % places
        found = jnp.where(here, jnp.where(slot < places, returned[:, :1], returned[:, 1:2]), 0.0)
        weight = weight_ref[k : k + 1, :].astype(jnp.bfloat16).astype(jnp.float32)
        out_ref[k : k + 1, :] = jnp.sum(found, axis=0, keepdims=True) / weight


def grad_kernel(
    _, arrived_ref, marks_ref, hidden_ref, twin_hidden_ref, out_ref, order_ref, rows_ref, own_ref, *, first
):
    places = marks_ref.shape[0]
    pair_rows = arrived_ref.shape[1]

    @pl.when(pl.program_id(0) == 0)
    def _():
        size = places // 2 * pair_rows
        blocks = in_place(arrived_ref, 0, places) + in_place(arrived_ref, places, places)
        for number, block in enumerate(blocks):
            rows_ref[number * size : (number + 1) * size, :] = block.reshape(size, block.shape[2])
        marks = in_place(marks_ref, 0, places)
        for number in range(4):
            half = number // 2
            mark = jnp.broadcast_to(
                marks[number % 2][:, first + half : first + half + 1], (places // 2, own_ref.shape[1])
            )
            for p in range(pair_rows):
                own_ref[pl.ds(number * size + p, places // 2, stride=pair_rows), :] = mark
        order_ref[...] = jnp.zeros_like(order_ref)

    own = own_ref[:, :1] > 0.5
    hidden = jnp.where(own, hidden_ref[...], twin_hidden_ref[...])
    out_ref[...] = lax.dot_general(
        hidden, rows_ref[...], (((0,), (0,)), ((), ())), preferred_element_type=jnp.float32
    ).astype(out_ref.dtype)


def on_device(out_grad, route_weight, expert_ids, slot_expert, replica_pick, saved_gu, down_weight):
    ep = ("half", "place")
    sources = lax.axis_size(ep)
    places, copies = lax.axis_size("place"), lax.axis_size("rep")
    token_count, top_count = expert_ids.shape
    slot_count = slot_expert.shape[0]
    rows_total = saved_gu.shape[1]
    pair_rows = rows_total // sources
    features = out_grad.shape[1]
    hidden_units = down_weight.shape[1]
    ids_t = expert_ids.T
    weight_t = route_weight.T
    send_rows, target = pl.pallas_call(
        pack_kernel,
        out_shape=(
            jax.ShapeDtypeStruct((slot_count, pair_rows, features), jnp.bfloat16),
            jax.ShapeDtypeStruct((top_count, token_count), jnp.int32),
        ),
        name="pack",
    )(ids_t, weight_t, slot_expert[None], replica_pick, out_grad)
    around = [(i + places // 2) % places for i in range(places)]
    arrived = lax.all_to_all(
        send_rows,
        ep,
        split_axis=0,
        concat_axis=0,
        axis_index_groups=[around + [places + i for i in around]],
        tiled=True,
    )
    marked = 2 * pair_rows
    part = pl.pallas_call(
        hidden_kernel,
        out_shape=jax.ShapeDtypeStruct((rows_total, saved_gu.shape[3]), jnp.bfloat16),
        name="hidden",
    )(saved_gu[0])
    swap = [(0, 1), (1, 0)]
    marks = pl.pallas_call(
        functools.partial(mark_kernel, first=marked),
        in_specs=[pl.BlockSpec(memory_space=pltpu.VMEM)] * 3,
        out_shape=jax.ShapeDtypeStruct((places, slot_count), jnp.float32),
        scratch_shapes=[pltpu.VMEM((slot_count, slot_count), jnp.float32)],
        compiler_params=pltpu.CompilerParams(vmem_limit_bytes=4 << 20),
        name="marks",
    )(replica_pick, lax.ppermute(replica_pick, "half", swap), slot_expert[None])
    hidden = lax.all_gather(part, "rep", axis=1, tiled=True)
    twin_hidden = lax.ppermute(hidden, "half", swap)
    outputs = pl.pallas_call(
        forward_kernel,
        out_shape=pltpu.VMEM((rows_total, features), jnp.float32),
        compiler_params=pltpu.CompilerParams(vmem_limit_bytes=12 << 20),
        name="forward",
    )(hidden, down_weight[0])
    dots = pl.pallas_call(
        dots_kernel,
        in_specs=[pl.BlockSpec(memory_space=pltpu.VMEM)] * 3,
        out_shape=jax.ShapeDtypeStruct((places, 128), jnp.float32),
        scratch_shapes=[pltpu.VMEM((rows_total, 128), jnp.float32)],
        compiler_params=pltpu.CompilerParams(vmem_limit_bytes=8 << 20),
        name="dots",
    )(arrived, outputs, marks)
    met = lax.all_to_all(
        dots.reshape(places, 1, 128),
        "place",
        split_axis=0,
        concat_axis=0,
        axis_index_groups=[around],
        tiled=True,
    ).reshape(places, 128)
    group = 2 * copies
    turned = pl.pallas_call(
        functools.partial(turn_kernel, pair_rows=pair_rows, copies=copies),
        out_shape=jax.ShapeDtypeStruct((group, 128), jnp.float32),
        scratch_shapes=[pltpu.VMEM((128, 128), jnp.float32)],
        compiler_params=pltpu.CompilerParams(vmem_limit_bytes=4 << 20),
        name="turn",
    )(met)
    returned = lax.all_to_all(
        turned.reshape(group, 1, 128),
        ("half", "rep"),
        split_axis=0,
        concat_axis=0,
        tiled=True,
    )
    steps = 2
    block = hidden_units // steps
    down_grad, order = pl.pallas_call(
        functools.partial(grad_kernel, first=marked),
        grid=(steps,),
        in_specs=[
            pl.BlockSpec(memory_space=pl.ANY),
            pl.BlockSpec(arrived.shape, lambda i: (0, 0, 0)),
            pl.BlockSpec((places, 128), lambda i: (0, 0)),
            pl.BlockSpec((rows_total, block), lambda i: (0, i)),
            pl.BlockSpec((rows_total, block), lambda i: (0, i)),
        ],
        out_specs=(
            pl.BlockSpec((block, features), lambda i: (i, 0)),
            pl.BlockSpec((8, 128), lambda i: (0, 0)),
        ),
        out_shape=(
            jax.ShapeDtypeStruct((hidden_units, features), jnp.bfloat16),
            jax.ShapeDtypeStruct((8, 128), jnp.float32),
        ),
        scratch_shapes=[
            pltpu.VMEM((rows_total, features), jnp.bfloat16),
            pltpu.VMEM((rows_total, 128), jnp.float32),
        ],
        compiler_params=pltpu.CompilerParams(vmem_limit_bytes=24 << 20),
        name="down_grad",
    )(turned, arrived, met, hidden, twin_hidden)
    route_grad = pl.pallas_call(
        functools.partial(pick_kernel, places=places, copies=copies),
        in_specs=[pl.BlockSpec(memory_space=pltpu.VMEM)] * 3 + [pl.BlockSpec(memory_space=pl.ANY)],
        out_shape=jax.ShapeDtypeStruct((top_count, token_count), jnp.float32),
        scratch_shapes=[pltpu.VMEM((128, 128), jnp.float32)],
        compiler_params=pltpu.CompilerParams(vmem_limit_bytes=4 << 20),
        name="pick",
    )(returned.reshape(group, 128), target, weight_t, order)
    return (down_grad[None], route_grad.T)


def solution(mesh):
    ep, rep = mesh.shape["ep"], mesh.shape["rep"]
    halves = Mesh(mesh.devices.reshape(2, ep // 2, rep), ("half", "place", "rep"))
    ep = ("half", "place")
    placed = (
        P(ep, "rep"),
        P(ep, None),
        P(ep, None),
        P(),
        P(ep, None),
        P(ep, None, None, "rep"),
        P(ep, None, "rep"),
    )
    return jax.shard_map(
        on_device,
        mesh=halves,
        in_specs=placed,
        out_specs=(P(ep, None, "rep"), P(ep, None)),
        check_vma=False,
    )
```

```python
import functools

import jax
import jax.numpy as jnp
from jax import lax
from jax.experimental import pallas as pl
from jax.experimental.pallas import tpu as pltpu
from jax.sharding import Mesh, PartitionSpec as P


def pack_kernel(ids_ref, weight_ref, slot_expert_ref, pick_ref, grad_ref, rows_ref, target_ref):
    top, tokens = ids_ref.shape
    experts = pick_ref.shape[1]
    slots, pair_rows, _ = rows_ref.shape
    slot_expert = slot_expert_ref[...]
    lane = lax.broadcasted_iota(jnp.int32, (1, slots), 1)
    twin = pltpu.roll(slot_expert, slots // 2, 1)
    shared = jnp.where(twin == slot_expert, 1, 0)
    rank = jnp.where((lane >= slots // 2) & (shared > 0), 1.0, 0.0)
    holds = lax.broadcasted_iota(jnp.int32, (experts, slots), 0) == slot_expert
    pick = jnp.dot(
        pick_ref[...].astype(jnp.bfloat16),
        jnp.where(holds, 1.0, 0.0).astype(jnp.bfloat16),
        preferred_element_type=jnp.float32,
    )
    picked = pick == rank
    serves = holds & picked
    slot_of = jnp.sum(jnp.where(serves, lane, 0).astype(jnp.float32), axis=1, keepdims=True)
    other = jnp.where(shared > 0, jnp.where(lane < slots // 2, slots // 2, -(slots // 2)), 0)
    twin_of = slot_of + jnp.sum(
        jnp.where(serves, other, 0).astype(jnp.float32), axis=1, keepdims=True
    )
    expert = lax.broadcasted_iota(jnp.int32, (experts, tokens), 0)
    chosen = [expert == ids_ref[k : k + 1, :] for k in range(top)]
    named = sum(jnp.where(c, 1.0, 0.0) for c in chosen)
    earlier = lax.broadcasted_iota(jnp.int32, (tokens, tokens), 0) < lax.broadcasted_iota(
        jnp.int32, (tokens, tokens), 1
    )
    before = jnp.dot(
        named.astype(jnp.bfloat16),
        jnp.where(earlier, 1.0, 0.0).astype(jnp.bfloat16),
        preferred_element_type=jnp.float32,
    )
    place = slot_of * pair_rows + before
    twin_place = twin_of * pair_rows + before
    row = lax.broadcasted_iota(jnp.int32, (slots * pair_rows, tokens), 0) ^ (slots // 4 * pair_rows)
    mix = jnp.zeros((slots * pair_rows, tokens), jnp.float32)
    for k in range(top):
        target = jnp.sum(jnp.where(chosen[k], place, 0.0), axis=0, keepdims=True).astype(jnp.int32)
        twin_target = jnp.sum(jnp.where(chosen[k], twin_place, 0.0), axis=0, keepdims=True)
        target_ref[k : k + 1, :] = target
        here = (row == target) | (row == twin_target.astype(jnp.int32))
        mix += jnp.where(here, weight_ref[k : k + 1, :], 0.0)
    rows = jnp.dot(mix.astype(jnp.bfloat16), grad_ref[...], preferred_element_type=jnp.float32)
    rows_ref[...] = rows.astype(rows_ref.dtype).reshape(rows_ref.shape)


def in_place(ref, start, count):
    middle = count // 2
    return [ref[start + middle : start + count], ref[start : start + middle]]


def hidden_kernel(saved_ref, out_ref):
    gate = saved_ref[:, 0, :].astype(jnp.float32)
    up = saved_ref[:, 1, :].astype(jnp.float32)
    out_ref[...] = (gate / (1.0 + jnp.exp(-gate)) * up).astype(out_ref.dtype)


def mark_kernel(pick_ref, twin_ref, slot_expert_ref, out_ref, scratch, *, first):
    experts = pick_ref.shape[1]
    slots = slot_expert_ref.shape[1]
    slot_expert = slot_expert_ref[...]
    lane = lax.broadcasted_iota(jnp.int32, (1, slots), 1)
    twin = pltpu.roll(slot_expert, slots // 2, 1)
    rank = jnp.where((lane >= slots // 2) & (twin == slot_expert), 1.0, 0.0)
    holds = lax.broadcasted_iota(jnp.int32, (experts, slots), 0) == slot_expert
    holds = jnp.where(holds, 1.0, 0.0).astype(jnp.bfloat16)
    half = lax.axis_index("half")
    own, other = (
        jnp.dot(ref[...].astype(jnp.bfloat16), holds, preferred_element_type=jnp.float32)
        for ref in (pick_ref, twin_ref)
    )
    scratch[...] = jnp.zeros_like(scratch)
    for source in range(2):
        pick = jnp.where(half == source, own, other)
        scratch[source : source + 1, :] = jnp.where(pick == rank, 1.0, 0.0)
    scratch[...] = scratch[...].T
    places = out_ref.shape[0]
    held = scratch[pl.ds(pl.multiple_of(half * places, places), places), :]
    out_ref[...] = pltpu.roll(held, first, 1)


def pass_kernel(hidden_ref, _, out_ref):
    out_ref[...] = hidden_ref[...]


def forward_kernel(hidden_ref, weight_ref, out_ref):
    out_ref[...] = jnp.dot(hidden_ref[...], weight_ref[...], preferred_element_type=jnp.float32)


def dots_kernel(arrived_ref, outputs_ref, marks_ref, dots_ref, scratch):
    places = dots_ref.shape[0]
    pair_rows, features = arrived_ref.shape[1:]
    size = places // 2 * pair_rows
    blocks = in_place(arrived_ref, 0, places) + in_place(arrived_ref, places, places)
    for number, block in enumerate(blocks):
        here = slice(number * size, (number + 1) * size)
        rows = block.reshape(size, features).astype(jnp.float32)
        total = jnp.sum(rows * outputs_ref[here, :], axis=1, keepdims=True)
        scratch[here, :] = jnp.broadcast_to(total, (size, scratch.shape[1]))
    lane = lax.broadcasted_iota(jnp.int32, dots_ref.shape, 1)
    found = marks_ref[...]
    for half in range(2):
        for p in range(pair_rows):
            part = scratch[pl.ds(half * places * pair_rows + p, places, stride=pair_rows), :]
            found = jnp.where(lane == half * pair_rows + p, part, found)
    dots_ref[: places // 2, :] = found[places // 2 :, :]
    dots_ref[places // 2 :, :] = found[: places // 2, :]


def turn_kernel(arrived_ref, out_ref, scratch, *, pair_rows, copies):
    places = arrived_ref.shape[0]
    scratch[...] = jnp.zeros_like(scratch)
    for number, block in enumerate(in_place(arrived_ref, 0, places)):
        scratch[number * places // 2 : (number + 1) * places // 2, :] = block
    turned = scratch[...].T
    for half in range(2):
        row = turned[half * pair_rows : half * pair_rows + 1, :]
        for p in range(1, pair_rows):
            other = turned[half * pair_rows + p : half * pair_rows + p + 1, :]
            row += pltpu.roll(other, p * places, 1)
        out_ref[half * copies : (half + 1) * copies, :] = jnp.broadcast_to(
            row, (copies, out_ref.shape[1])
        )


def pick_kernel(returned_ref, target_ref, weight_ref, _, out_ref, scratch, *, places, copies):
    top, tokens = target_ref.shape
    pair_rows = 2
    scratch[...] = jnp.zeros_like(scratch)
    for half in range(2):
        scratch[half : half + 1, :] = jnp.sum(
            returned_ref[half * copies : (half + 1) * copies, :], axis=0, keepdims=True
        )
    returned = scratch[...].T
    row = lax.broadcasted_iota(jnp.int32, (returned.shape[0], tokens), 0)
    for k in range(top):
        target = target_ref[k : k + 1, :]
        slot = target // pair_rows
        here = row == (target % pair_rows) * places + slot % places
        found = jnp.where(here, jnp.where(slot < places, returned[:, :1], returned[:, 1:2]), 0.0)
        weight = weight_ref[k : k + 1, :].astype(jnp.bfloat16).astype(jnp.float32)
        out_ref[k : k + 1, :] = jnp.sum(found, axis=0, keepdims=True) / weight


def grad_kernel(
    _, arrived_ref, marks_ref, hidden_ref, twin_hidden_ref, out_ref, order_ref, rows_ref, own_ref, *, first
):
    places = marks_ref.shape[0]
    pair_rows = arrived_ref.shape[1]

    @pl.when(pl.program_id(0) == 0)
    def _():
        size = places // 2 * pair_rows
        blocks = in_place(arrived_ref, 0, places) + in_place(arrived_ref, places, places)
        for number, block in enumerate(blocks):
            rows_ref[number * size : (number + 1) * size, :] = block.reshape(size, block.shape[2])
        marks = in_place(marks_ref, 0, places)
        for number in range(4):
            half = number // 2
            mark = jnp.broadcast_to(
                marks[number % 2][:, first + half : first + half + 1], (places // 2, own_ref.shape[1])
            )
            for p in range(pair_rows):
                own_ref[pl.ds(number * size + p, places // 2, stride=pair_rows), :] = mark
        order_ref[...] = jnp.zeros_like(order_ref)

    own = own_ref[:, :1] > 0.5
    hidden = jnp.where(own, hidden_ref[...], twin_hidden_ref[...])
    out_ref[...] = lax.dot_general(
        hidden, rows_ref[...], (((0,), (0,)), ((), ())), preferred_element_type=jnp.float32
    ).astype(out_ref.dtype)


def on_device(out_grad, route_weight, expert_ids, slot_expert, replica_pick, saved_gu, down_weight):
    ep = ("half", "place")
    sources = lax.axis_size(ep)
    places, copies = lax.axis_size("place"), lax.axis_size("rep")
    token_count, top_count = expert_ids.shape
    slot_count = slot_expert.shape[0]
    rows_total = saved_gu.shape[1]
    pair_rows = rows_total // sources
    features = out_grad.shape[1]
    hidden_units = down_weight.shape[1]
    ids_t = expert_ids.T
    weight_t = route_weight.T
    send_rows, target = pl.pallas_call(
        pack_kernel,
        out_shape=(
            jax.ShapeDtypeStruct((slot_count, pair_rows, features), jnp.bfloat16),
            jax.ShapeDtypeStruct((top_count, token_count), jnp.int32),
        ),
        name="pack",
    )(ids_t, weight_t, slot_expert[None], replica_pick, out_grad)
    around = [(i + places // 2) % places for i in range(places)]
    arrived = lax.all_to_all(
        send_rows,
        ep,
        split_axis=0,
        concat_axis=0,
        axis_index_groups=[around + [places + i for i in around]],
        tiled=True,
    )
    marked = 2 * pair_rows
    part = pl.pallas_call(
        hidden_kernel,
        out_shape=jax.ShapeDtypeStruct((rows_total, saved_gu.shape[3]), jnp.bfloat16),
        compiler_params=pltpu.CompilerParams(vmem_limit_bytes=8 << 20),
        name="hidden",
    )(saved_gu[0])
    swap = [(0, 1), (1, 0)]
    marks = pl.pallas_call(
        functools.partial(mark_kernel, first=marked),
        in_specs=[pl.BlockSpec(memory_space=pltpu.VMEM)] * 3,
        out_shape=jax.ShapeDtypeStruct((places, slot_count), jnp.float32),
        scratch_shapes=[pltpu.VMEM((slot_count, slot_count), jnp.float32)],
        compiler_params=pltpu.CompilerParams(vmem_limit_bytes=4 << 20),
        name="marks",
    )(replica_pick, lax.ppermute(replica_pick, "half", swap), slot_expert[None])
    hidden = lax.all_gather(part, "rep", axis=1, tiled=True)
    outputs = pl.pallas_call(
        forward_kernel,
        out_shape=pltpu.VMEM((rows_total, features), jnp.float32),
        compiler_params=pltpu.CompilerParams(vmem_limit_bytes=12 << 20),
        name="forward",
    )(hidden, down_weight[0])
    sent = pl.pallas_call(
        pass_kernel,
        in_specs=[pl.BlockSpec(memory_space=pltpu.VMEM), pl.BlockSpec(memory_space=pl.ANY)],
        out_shape=jax.ShapeDtypeStruct(hidden.shape, hidden.dtype),
        compiler_params=pltpu.CompilerParams(vmem_limit_bytes=4 << 20),
        name="pass",
    )(hidden, marks)
    twin_hidden = lax.ppermute(sent, "half", swap)
    dots = pl.pallas_call(
        dots_kernel,
        in_specs=[pl.BlockSpec(memory_space=pltpu.VMEM)] * 3,
        out_shape=jax.ShapeDtypeStruct((places, 128), jnp.float32),
        scratch_shapes=[pltpu.VMEM((rows_total, 128), jnp.float32)],
        compiler_params=pltpu.CompilerParams(vmem_limit_bytes=8 << 20),
        name="dots",
    )(arrived, outputs, marks)
    met = lax.all_to_all(
        dots.reshape(places, 1, 128),
        "place",
        split_axis=0,
        concat_axis=0,
        axis_index_groups=[around],
        tiled=True,
    ).reshape(places, 128)
    group = 2 * copies
    turned = pl.pallas_call(
        functools.partial(turn_kernel, pair_rows=pair_rows, copies=copies),
        out_shape=jax.ShapeDtypeStruct((group, 128), jnp.float32),
        scratch_shapes=[pltpu.VMEM((128, 128), jnp.float32)],
        compiler_params=pltpu.CompilerParams(vmem_limit_bytes=4 << 20),
        name="turn",
    )(met)
    returned = lax.all_to_all(
        turned.reshape(group, 1, 128),
        ("half", "rep"),
        split_axis=0,
        concat_axis=0,
        tiled=True,
    )
    steps = 2
    block = hidden_units // steps
    down_grad, order = pl.pallas_call(
        functools.partial(grad_kernel, first=marked),
        grid=(steps,),
        in_specs=[
            pl.BlockSpec(memory_space=pl.ANY),
            pl.BlockSpec(arrived.shape, lambda i: (0, 0, 0)),
            pl.BlockSpec((places, 128), lambda i: (0, 0)),
            pl.BlockSpec((rows_total, block), lambda i: (0, i)),
            pl.BlockSpec((rows_total, block), lambda i: (0, i)),
        ],
        out_specs=(
            pl.BlockSpec((block, features), lambda i: (i, 0)),
            pl.BlockSpec((8, 128), lambda i: (0, 0)),
        ),
        out_shape=(
            jax.ShapeDtypeStruct((hidden_units, features), jnp.bfloat16),
            jax.ShapeDtypeStruct((8, 128), jnp.float32),
        ),
        scratch_shapes=[
            pltpu.VMEM((rows_total, features), jnp.bfloat16),
            pltpu.VMEM((rows_total, 128), jnp.float32),
        ],
        compiler_params=pltpu.CompilerParams(vmem_limit_bytes=24 << 20),
        name="down_grad",
    )(turned, arrived, met, hidden, twin_hidden)
    route_grad = pl.pallas_call(
        functools.partial(pick_kernel, places=places, copies=copies),
        in_specs=[pl.BlockSpec(memory_space=pltpu.VMEM)] * 3 + [pl.BlockSpec(memory_space=pl.ANY)],
        out_shape=jax.ShapeDtypeStruct((top_count, token_count), jnp.float32),
        scratch_shapes=[pltpu.VMEM((128, 128), jnp.float32)],
        compiler_params=pltpu.CompilerParams(vmem_limit_bytes=4 << 20),
        name="pick",
    )(returned.reshape(group, 128), target, weight_t, order)
    return (down_grad[None], route_grad.T)


def solution(mesh):
    ep, rep = mesh.shape["ep"], mesh.shape["rep"]
    halves = Mesh(mesh.devices.reshape(2, ep // 2, rep), ("half", "place", "rep"))
    ep = ("half", "place")
    placed = (
        P(ep, "rep"),
        P(ep, None),
        P(ep, None),
        P(),
        P(ep, None),
        P(ep, None, None, "rep"),
        P(ep, None, "rep"),
    )
    return jax.shard_map(
        on_device,
        mesh=halves,
        in_specs=placed,
        out_specs=(P(ep, None, "rep"), P(ep, None)),
        check_vma=False,
    )
```

```python
import functools

import jax
import jax.numpy as jnp
from jax import lax
from jax.experimental import pallas as pl
from jax.experimental.pallas import tpu as pltpu
from jax.sharding import Mesh, PartitionSpec as P


DISPATCH_FIRST = 114
PLACE_FIRST = 34
LINE_FIRST = 4


def turned_order(count, first):
    return [[m ^ first for m in range(count)]]


def sources_of(ref):
    step = DISPATCH_FIRST & -DISPATCH_FIRST
    return jnp.concatenate(
        [ref[k ^ DISPATCH_FIRST : (k ^ DISPATCH_FIRST) + step] for k in range(0, ref.shape[0], step)],
        axis=0,
    )


def swap_places(rows):
    count = rows.shape[0]
    row = lax.broadcasted_iota(jnp.int32, rows.shape, 0)
    for bit in (b for b in (1, 2, 4, 8, 16, 32) if b & PLACE_FIRST):
        rows = jnp.where(row & bit == 0, pltpu.roll(rows, count - bit, 0), pltpu.roll(rows, bit, 0))
    return rows


def pack_kernel(ids_ref, weight_ref, slot_expert_ref, pick_ref, grad_ref, rows_ref, target_ref):
    top, tokens = ids_ref.shape
    experts = pick_ref.shape[1]
    slots, pair_rows, _ = rows_ref.shape
    slot_expert = slot_expert_ref[...]
    lane = lax.broadcasted_iota(jnp.int32, (1, slots), 1)
    twin = pltpu.roll(slot_expert, slots // 2, 1)
    shared = jnp.where(twin == slot_expert, 1, 0)
    rank = jnp.where((lane >= slots // 2) & (shared > 0), 1.0, 0.0)
    holds = lax.broadcasted_iota(jnp.int32, (experts, slots), 0) == slot_expert
    pick = jnp.dot(
        pick_ref[...].astype(jnp.bfloat16),
        jnp.where(holds, 1.0, 0.0).astype(jnp.bfloat16),
        preferred_element_type=jnp.float32,
    )
    picked = pick == rank
    serves = holds & picked
    slot_of = jnp.sum(jnp.where(serves, lane, 0).astype(jnp.float32), axis=1, keepdims=True)
    other = jnp.where(shared > 0, jnp.where(lane < slots // 2, slots // 2, -(slots // 2)), 0)
    twin_of = slot_of + jnp.sum(
        jnp.where(serves, other, 0).astype(jnp.float32), axis=1, keepdims=True
    )
    expert = lax.broadcasted_iota(jnp.int32, (experts, tokens), 0)
    chosen = [expert == ids_ref[k : k + 1, :] for k in range(top)]
    named = sum(jnp.where(c, 1.0, 0.0) for c in chosen)
    earlier = lax.broadcasted_iota(jnp.int32, (tokens, tokens), 0) < lax.broadcasted_iota(
        jnp.int32, (tokens, tokens), 1
    )
    before = jnp.dot(
        named.astype(jnp.bfloat16),
        jnp.where(earlier, 1.0, 0.0).astype(jnp.bfloat16),
        preferred_element_type=jnp.float32,
    )
    place = slot_of * pair_rows + before
    twin_place = twin_of * pair_rows + before
    row = lax.broadcasted_iota(jnp.int32, (slots * pair_rows, tokens), 0)
    row = row ^ (DISPATCH_FIRST * pair_rows)
    mix = jnp.zeros((slots * pair_rows, tokens), jnp.float32)
    for k in range(top):
        target = jnp.sum(jnp.where(chosen[k], place, 0.0), axis=0, keepdims=True).astype(jnp.int32)
        twin_target = jnp.sum(jnp.where(chosen[k], twin_place, 0.0), axis=0, keepdims=True)
        target_ref[k : k + 1, :] = target
        here = (row == target) | (row == twin_target.astype(jnp.int32))
        mix += jnp.where(here, weight_ref[k : k + 1, :], 0.0)
    rows = jnp.dot(mix.astype(jnp.bfloat16), grad_ref[...], preferred_element_type=jnp.float32)
    rows_ref[...] = rows.astype(rows_ref.dtype).reshape(rows_ref.shape)


def hidden_kernel(saved_ref, out_ref):
    gate = saved_ref[:, 0, :].astype(jnp.float32)
    up = saved_ref[:, 1, :].astype(jnp.float32)
    out_ref[...] = (gate / (1.0 + jnp.exp(-gate)) * up).astype(out_ref.dtype)


def mark_kernel(pick_ref, twin_ref, slot_expert_ref, out_ref, scratch, *, first):
    experts = pick_ref.shape[1]
    slots = slot_expert_ref.shape[1]
    slot_expert = slot_expert_ref[...]
    lane = lax.broadcasted_iota(jnp.int32, (1, slots), 1)
    twin = pltpu.roll(slot_expert, slots // 2, 1)
    rank = jnp.where((lane >= slots // 2) & (twin == slot_expert), 1.0, 0.0)
    holds = lax.broadcasted_iota(jnp.int32, (experts, slots), 0) == slot_expert
    holds = jnp.where(holds, 1.0, 0.0).astype(jnp.bfloat16)
    half = lax.axis_index("half")
    own, other = (
        jnp.dot(ref[...].astype(jnp.bfloat16), holds, preferred_element_type=jnp.float32)
        for ref in (pick_ref, twin_ref)
    )
    scratch[...] = jnp.zeros_like(scratch)
    for source in range(2):
        pick = jnp.where(half == source, own, other)
        scratch[source : source + 1, :] = jnp.where(pick == rank, 1.0, 0.0)
    scratch[...] = scratch[...].T
    places = out_ref.shape[0]
    held = scratch[pl.ds(pl.multiple_of(half * places, places), places), :]
    out_ref[...] = pltpu.roll(held, first, 1)


def pass_kernel(hidden_ref, _, out_ref):
    out_ref[...] = hidden_ref[...]


def forward_kernel(hidden_ref, weight_ref, out_ref):
    out_ref[...] = jnp.dot(hidden_ref[...], weight_ref[...], preferred_element_type=jnp.float32)


def dots_kernel(arrived_ref, outputs_ref, marks_ref, dots_ref, scratch):
    places = dots_ref.shape[0]
    pair_rows = arrived_ref.shape[1]
    rows = sources_of(arrived_ref).reshape(outputs_ref.shape)
    total = jnp.sum(rows.astype(jnp.float32) * outputs_ref[...], axis=1, keepdims=True)
    scratch[...] = jnp.broadcast_to(total, scratch.shape)
    lane = lax.broadcasted_iota(jnp.int32, dots_ref.shape, 1)
    found = marks_ref[...]
    for half in range(2):
        for p in range(pair_rows):
            part = scratch[pl.ds(half * places * pair_rows + p, places, stride=pair_rows), :]
            found = jnp.where(lane == half * pair_rows + p, part, found)
    dots_ref[...] = swap_places(found)


def turn_kernel(arrived_ref, out_ref, scratch, *, pair_rows, copies):
    places = arrived_ref.shape[0]
    scratch[...] = jnp.zeros_like(scratch)
    scratch[:places, :] = arrived_ref[...]
    turned = scratch[...].T
    for half in range(2):
        row = turned[half * pair_rows : half * pair_rows + 1, :]
        for p in range(1, pair_rows):
            other = turned[half * pair_rows + p : half * pair_rows + p + 1, :]
            row += pltpu.roll(other, p * places, 1)
        start = half * copies ^ LINE_FIRST
        out_ref[start : start + copies, :] = jnp.broadcast_to(row, (copies, out_ref.shape[1]))


def pick_kernel(returned_ref, target_ref, weight_ref, _, out_ref, scratch, *, places, copies):
    top, tokens = target_ref.shape
    pair_rows = 2
    scratch[...] = jnp.zeros_like(scratch)
    for half in range(2):
        start = half * copies ^ LINE_FIRST
        scratch[half : half + 1, :] = jnp.sum(
            returned_ref[start : start + copies, :], axis=0, keepdims=True
        )
    returned = scratch[...].T
    row = lax.broadcasted_iota(jnp.int32, (returned.shape[0], tokens), 0)
    for k in range(top):
        target = target_ref[k : k + 1, :]
        slot = target // pair_rows
        here = row == (target % pair_rows) * places + (slot % places ^ PLACE_FIRST)
        found = jnp.where(here, jnp.where(slot < places, returned[:, :1], returned[:, 1:2]), 0.0)
        weight = weight_ref[k : k + 1, :].astype(jnp.bfloat16).astype(jnp.float32)
        out_ref[k : k + 1, :] = jnp.sum(found, axis=0, keepdims=True) / weight


def grad_kernel(
    _, arrived_ref, marks_ref, hidden_ref, twin_hidden_ref, out_ref, order_ref, rows_ref, own_ref, *, first
):
    places = marks_ref.shape[0]
    pair_rows = arrived_ref.shape[1]

    @pl.when(pl.program_id(0) == 0)
    def _():
        rows_ref[...] = sources_of(arrived_ref).reshape(rows_ref.shape)
        marks = swap_places(marks_ref[...])
        for half in range(2):
            mark = jnp.broadcast_to(marks[:, first + half : first + half + 1], marks.shape)
            for p in range(pair_rows):
                own_ref[pl.ds(half * places * pair_rows + p, places, stride=pair_rows), :] = mark
        order_ref[...] = jnp.zeros_like(order_ref)

    own = own_ref[:, :1] > 0.5
    hidden = jnp.where(own, hidden_ref[...], twin_hidden_ref[...])
    out_ref[...] = lax.dot_general(
        hidden, rows_ref[...], (((0,), (0,)), ((), ())), preferred_element_type=jnp.float32
    ).astype(out_ref.dtype)


def on_device(out_grad, route_weight, expert_ids, slot_expert, replica_pick, saved_gu, down_weight):
    ep = ("half", "place")
    sources = lax.axis_size(ep)
    places, copies = lax.axis_size("place"), lax.axis_size("rep")
    token_count, top_count = expert_ids.shape
    slot_count = slot_expert.shape[0]
    rows_total = saved_gu.shape[1]
    pair_rows = rows_total // sources
    features = out_grad.shape[1]
    hidden_units = down_weight.shape[1]
    ids_t = expert_ids.T
    weight_t = route_weight.T
    send_rows, target = pl.pallas_call(
        pack_kernel,
        out_shape=(
            jax.ShapeDtypeStruct((slot_count, pair_rows, features), jnp.bfloat16),
            jax.ShapeDtypeStruct((top_count, token_count), jnp.int32),
        ),
        name="pack",
    )(ids_t, weight_t, slot_expert[None], replica_pick, out_grad)
    arrived = lax.all_to_all(
        send_rows,
        ep,
        split_axis=0,
        concat_axis=0,
        axis_index_groups=turned_order(sources, DISPATCH_FIRST),
        tiled=True,
    )
    marked = 2 * pair_rows
    part = pl.pallas_call(
        hidden_kernel,
        out_shape=jax.ShapeDtypeStruct((rows_total, saved_gu.shape[3]), jnp.bfloat16),
        compiler_params=pltpu.CompilerParams(vmem_limit_bytes=8 << 20),
        name="hidden",
    )(saved_gu[0])
    swap = [(0, 1), (1, 0)]
    marks = pl.pallas_call(
        functools.partial(mark_kernel, first=marked),
        in_specs=[pl.BlockSpec(memory_space=pltpu.VMEM)] * 3,
        out_shape=jax.ShapeDtypeStruct((places, slot_count), jnp.float32),
        scratch_shapes=[pltpu.VMEM((slot_count, slot_count), jnp.float32)],
        compiler_params=pltpu.CompilerParams(vmem_limit_bytes=4 << 20),
        name="marks",
    )(replica_pick, lax.ppermute(replica_pick, "half", swap), slot_expert[None])
    hidden = lax.all_gather(part, "rep", axis=1, tiled=True)
    outputs = pl.pallas_call(
        forward_kernel,
        out_shape=pltpu.VMEM((rows_total, features), jnp.float32),
        compiler_params=pltpu.CompilerParams(vmem_limit_bytes=12 << 20),
        name="forward",
    )(hidden, down_weight[0])
    sent = pl.pallas_call(
        pass_kernel,
        in_specs=[pl.BlockSpec(memory_space=pltpu.VMEM), pl.BlockSpec(memory_space=pl.ANY)],
        out_shape=jax.ShapeDtypeStruct(hidden.shape, hidden.dtype),
        compiler_params=pltpu.CompilerParams(vmem_limit_bytes=4 << 20),
        name="pass",
    )(hidden, marks)
    twin_hidden = lax.ppermute(sent, "half", swap)
    dots = pl.pallas_call(
        dots_kernel,
        in_specs=[pl.BlockSpec(memory_space=pltpu.VMEM)] * 3,
        out_shape=jax.ShapeDtypeStruct((places, 128), jnp.float32),
        scratch_shapes=[pltpu.VMEM((rows_total, 128), jnp.float32)],
        compiler_params=pltpu.CompilerParams(vmem_limit_bytes=8 << 20),
        name="dots",
    )(arrived, outputs, marks)
    met = lax.all_to_all(
        dots.reshape(places, 1, 128),
        "place",
        split_axis=0,
        concat_axis=0,
        axis_index_groups=turned_order(places, PLACE_FIRST),
        tiled=True,
    ).reshape(places, 128)
    group = 2 * copies
    turned = pl.pallas_call(
        functools.partial(turn_kernel, pair_rows=pair_rows, copies=copies),
        out_shape=jax.ShapeDtypeStruct((group, 128), jnp.float32),
        scratch_shapes=[pltpu.VMEM((128, 128), jnp.float32)],
        compiler_params=pltpu.CompilerParams(vmem_limit_bytes=4 << 20),
        name="turn",
    )(met)
    returned = lax.all_to_all(
        turned.reshape(group, 1, 128),
        ("half", "rep"),
        split_axis=0,
        concat_axis=0,
        axis_index_groups=turned_order(group, LINE_FIRST),
        tiled=True,
    )
    steps = 2
    block = hidden_units // steps
    down_grad, order = pl.pallas_call(
        functools.partial(grad_kernel, first=marked),
        grid=(steps,),
        in_specs=[
            pl.BlockSpec(memory_space=pl.ANY),
            pl.BlockSpec(arrived.shape, lambda i: (0, 0, 0)),
            pl.BlockSpec((places, 128), lambda i: (0, 0)),
            pl.BlockSpec((rows_total, block), lambda i: (0, i)),
            pl.BlockSpec((rows_total, block), lambda i: (0, i)),
        ],
        out_specs=(
            pl.BlockSpec((block, features), lambda i: (i, 0)),
            pl.BlockSpec((8, 128), lambda i: (0, 0)),
        ),
        out_shape=(
            jax.ShapeDtypeStruct((hidden_units, features), jnp.bfloat16),
            jax.ShapeDtypeStruct((8, 128), jnp.float32),
        ),
        scratch_shapes=[
            pltpu.VMEM((rows_total, features), jnp.bfloat16),
            pltpu.VMEM((rows_total, 128), jnp.float32),
        ],
        compiler_params=pltpu.CompilerParams(vmem_limit_bytes=24 << 20),
        name="down_grad",
    )(turned, arrived, met, hidden, twin_hidden)
    route_grad = pl.pallas_call(
        functools.partial(pick_kernel, places=places, copies=copies),
        in_specs=[pl.BlockSpec(memory_space=pltpu.VMEM)] * 3 + [pl.BlockSpec(memory_space=pl.ANY)],
        out_shape=jax.ShapeDtypeStruct((top_count, token_count), jnp.float32),
        scratch_shapes=[pltpu.VMEM((128, 128), jnp.float32)],
        compiler_params=pltpu.CompilerParams(vmem_limit_bytes=4 << 20),
        name="pick",
    )(returned.reshape(group, 128), target, weight_t, order)
    return (down_grad[None], route_grad.T)


def solution(mesh):
    ep, rep = mesh.shape["ep"], mesh.shape["rep"]
    halves = Mesh(mesh.devices.reshape(2, ep // 2, rep), ("half", "place", "rep"))
    ep = ("half", "place")
    placed = (
        P(ep, "rep"),
        P(ep, None),
        P(ep, None),
        P(),
        P(ep, None),
        P(ep, None, None, "rep"),
        P(ep, None, "rep"),
    )
    return jax.shard_map(
        on_device,
        mesh=halves,
        in_specs=placed,
        out_specs=(P(ep, None, "rep"), P(ep, None)),
        check_vma=False,
    )
```

```python
import functools

import jax
import jax.numpy as jnp
from jax import lax
from jax.experimental import pallas as pl
from jax.experimental.pallas import tpu as pltpu
from jax.sharding import Mesh, PartitionSpec as P


DISPATCH_FIRST = 106
PLACE_FIRST = 34
LINE_FIRST = 6


def turned_order(count, first):
    return [[m ^ first for m in range(count)]]


def sources_of(ref):
    step = DISPATCH_FIRST & -DISPATCH_FIRST
    return jnp.concatenate(
        [ref[k ^ DISPATCH_FIRST : (k ^ DISPATCH_FIRST) + step] for k in range(0, ref.shape[0], step)],
        axis=0,
    )


def swap_places(rows):
    count = rows.shape[0]
    row = lax.broadcasted_iota(jnp.int32, rows.shape, 0)
    for bit in (b for b in (1, 2, 4, 8, 16, 32) if b & PLACE_FIRST):
        rows = jnp.where(row & bit == 0, pltpu.roll(rows, count - bit, 0), pltpu.roll(rows, bit, 0))
    return rows


def pack_kernel(ids_ref, weight_ref, slot_expert_ref, pick_ref, grad_ref, rows_ref, target_ref):
    top, tokens = ids_ref.shape
    experts = pick_ref.shape[1]
    slots, pair_rows, _ = rows_ref.shape
    slot_expert = slot_expert_ref[...]
    lane = lax.broadcasted_iota(jnp.int32, (1, slots), 1)
    twin = pltpu.roll(slot_expert, slots // 2, 1)
    shared = jnp.where(twin == slot_expert, 1, 0)
    rank = jnp.where((lane >= slots // 2) & (shared > 0), 1.0, 0.0)
    holds = lax.broadcasted_iota(jnp.int32, (experts, slots), 0) == slot_expert
    pick = jnp.dot(
        pick_ref[...].astype(jnp.bfloat16),
        jnp.where(holds, 1.0, 0.0).astype(jnp.bfloat16),
        preferred_element_type=jnp.float32,
    )
    picked = pick == rank
    serves = holds & picked
    slot_of = jnp.sum(jnp.where(serves, lane, 0).astype(jnp.float32), axis=1, keepdims=True)
    other = jnp.where(shared > 0, jnp.where(lane < slots // 2, slots // 2, -(slots // 2)), 0)
    twin_of = slot_of + jnp.sum(
        jnp.where(serves, other, 0).astype(jnp.float32), axis=1, keepdims=True
    )
    expert = lax.broadcasted_iota(jnp.int32, (experts, tokens), 0)
    chosen = [expert == ids_ref[k : k + 1, :] for k in range(top)]
    named = sum(jnp.where(c, 1.0, 0.0) for c in chosen)
    earlier = lax.broadcasted_iota(jnp.int32, (tokens, tokens), 0) < lax.broadcasted_iota(
        jnp.int32, (tokens, tokens), 1
    )
    before = jnp.dot(
        named.astype(jnp.bfloat16),
        jnp.where(earlier, 1.0, 0.0).astype(jnp.bfloat16),
        preferred_element_type=jnp.float32,
    )
    place = slot_of * pair_rows + before
    twin_place = twin_of * pair_rows + before
    row = lax.broadcasted_iota(jnp.int32, (slots * pair_rows, tokens), 0)
    row = row ^ (DISPATCH_FIRST * pair_rows)
    mix = jnp.zeros((slots * pair_rows, tokens), jnp.float32)
    for k in range(top):
        target = jnp.sum(jnp.where(chosen[k], place, 0.0), axis=0, keepdims=True).astype(jnp.int32)
        twin_target = jnp.sum(jnp.where(chosen[k], twin_place, 0.0), axis=0, keepdims=True)
        target_ref[k : k + 1, :] = target
        here = (row == target) | (row == twin_target.astype(jnp.int32))
        mix += jnp.where(here, weight_ref[k : k + 1, :], 0.0)
    rows = jnp.dot(mix.astype(jnp.bfloat16), grad_ref[...], preferred_element_type=jnp.float32)
    rows_ref[...] = rows.astype(rows_ref.dtype).reshape(rows_ref.shape)


def hidden_kernel(saved_ref, out_ref):
    gate = saved_ref[:, 0, :].astype(jnp.float32)
    up = saved_ref[:, 1, :].astype(jnp.float32)
    out_ref[...] = (gate / (1.0 + jnp.exp(-gate)) * up).astype(out_ref.dtype)


def mark_kernel(pick_ref, twin_ref, slot_expert_ref, out_ref, scratch, *, first):
    experts = pick_ref.shape[1]
    slots = slot_expert_ref.shape[1]
    slot_expert = slot_expert_ref[...]
    lane = lax.broadcasted_iota(jnp.int32, (1, slots), 1)
    twin = pltpu.roll(slot_expert, slots // 2, 1)
    rank = jnp.where((lane >= slots // 2) & (twin == slot_expert), 1.0, 0.0)
    holds = lax.broadcasted_iota(jnp.int32, (experts, slots), 0) == slot_expert
    holds = jnp.where(holds, 1.0, 0.0).astype(jnp.bfloat16)
    half = lax.axis_index("half")
    own, other = (
        jnp.dot(ref[...].astype(jnp.bfloat16), holds, preferred_element_type=jnp.float32)
        for ref in (pick_ref, twin_ref)
    )
    scratch[...] = jnp.zeros_like(scratch)
    for source in range(2):
        pick = jnp.where(half == source, own, other)
        scratch[source : source + 1, :] = jnp.where(pick == rank, 1.0, 0.0)
    scratch[...] = scratch[...].T
    places = out_ref.shape[0]
    held = scratch[pl.ds(pl.multiple_of(half * places, places), places), :]
    out_ref[...] = pltpu.roll(held, first, 1)


def pass_kernel(hidden_ref, _, out_ref):
    out_ref[...] = hidden_ref[...]


def forward_kernel(hidden_ref, weight_ref, out_ref):
    out_ref[...] = jnp.dot(hidden_ref[...], weight_ref[...], preferred_element_type=jnp.float32)


def dots_kernel(arrived_ref, outputs_ref, marks_ref, dots_ref, scratch):
    places = dots_ref.shape[0]
    pair_rows = arrived_ref.shape[1]
    rows = sources_of(arrived_ref).reshape(outputs_ref.shape)
    total = jnp.sum(rows.astype(jnp.float32) * outputs_ref[...], axis=1, keepdims=True)
    scratch[...] = jnp.broadcast_to(total, scratch.shape)
    lane = lax.broadcasted_iota(jnp.int32, dots_ref.shape, 1)
    found = marks_ref[...]
    for half in range(2):
        for p in range(pair_rows):
            part = scratch[pl.ds(half * places * pair_rows + p, places, stride=pair_rows), :]
            found = jnp.where(lane == half * pair_rows + p, part, found)
    dots_ref[...] = swap_places(found)


def turn_kernel(arrived_ref, out_ref, scratch, *, pair_rows, copies):
    places = arrived_ref.shape[0]
    scratch[...] = jnp.zeros_like(scratch)
    scratch[:places, :] = arrived_ref[...]
    turned = scratch[...].T
    for half in range(2):
        row = turned[half * pair_rows : half * pair_rows + 1, :]
        for p in range(1, pair_rows):
            other = turned[half * pair_rows + p : half * pair_rows + p + 1, :]
            row += pltpu.roll(other, p * places, 1)
        start = half * copies ^ LINE_FIRST // copies * copies
        out_ref[start : start + copies, :] = jnp.broadcast_to(row, (copies, out_ref.shape[1]))


def pick_kernel(returned_ref, target_ref, weight_ref, _, out_ref, scratch, *, places, copies):
    top, tokens = target_ref.shape
    pair_rows = 2
    scratch[...] = jnp.zeros_like(scratch)
    for half in range(2):
        start = half * copies ^ LINE_FIRST // copies * copies
        scratch[half : half + 1, :] = jnp.sum(
            returned_ref[start : start + copies, :], axis=0, keepdims=True
        )
    returned = scratch[...].T
    row = lax.broadcasted_iota(jnp.int32, (returned.shape[0], tokens), 0)
    for k in range(top):
        target = target_ref[k : k + 1, :]
        slot = target // pair_rows
        here = row == (target % pair_rows) * places + (slot % places ^ PLACE_FIRST)
        found = jnp.where(here, jnp.where(slot < places, returned[:, :1], returned[:, 1:2]), 0.0)
        weight = weight_ref[k : k + 1, :].astype(jnp.bfloat16).astype(jnp.float32)
        out_ref[k : k + 1, :] = jnp.sum(found, axis=0, keepdims=True) / weight


def grad_kernel(
    _, arrived_ref, marks_ref, hidden_ref, twin_hidden_ref, out_ref, order_ref, rows_ref, own_ref, *, first
):
    places = marks_ref.shape[0]
    pair_rows = arrived_ref.shape[1]

    @pl.when(pl.program_id(0) == 0)
    def _():
        rows_ref[...] = sources_of(arrived_ref).reshape(rows_ref.shape)
        marks = swap_places(marks_ref[...])
        for half in range(2):
            mark = jnp.broadcast_to(marks[:, first + half : first + half + 1], marks.shape)
            for p in range(pair_rows):
                own_ref[pl.ds(half * places * pair_rows + p, places, stride=pair_rows), :] = mark
        order_ref[...] = jnp.zeros_like(order_ref)

    own = own_ref[:, :1] > 0.5
    block = out_ref.shape[0]
    here = pl.ds(pl.multiple_of(pl.program_id(0) * block, block), block)
    hidden = jnp.where(own, hidden_ref[:, here], twin_hidden_ref[:, here])
    out_ref[...] = lax.dot_general(
        hidden, rows_ref[...], (((0,), (0,)), ((), ())), preferred_element_type=jnp.float32
    ).astype(out_ref.dtype)


def on_device(out_grad, route_weight, expert_ids, slot_expert, replica_pick, saved_gu, down_weight):
    ep = ("half", "place")
    sources = lax.axis_size(ep)
    places, copies = lax.axis_size("place"), lax.axis_size("rep")
    token_count, top_count = expert_ids.shape
    slot_count = slot_expert.shape[0]
    rows_total = saved_gu.shape[1]
    pair_rows = rows_total // sources
    features = out_grad.shape[1]
    hidden_units = down_weight.shape[1]
    ids_t = expert_ids.T
    weight_t = route_weight.T
    send_rows, target = pl.pallas_call(
        pack_kernel,
        out_shape=(
            jax.ShapeDtypeStruct((slot_count, pair_rows, features), jnp.bfloat16),
            jax.ShapeDtypeStruct((top_count, token_count), jnp.int32),
        ),
        name="pack",
    )(ids_t, weight_t, slot_expert[None], replica_pick, out_grad)
    arrived = lax.all_to_all(
        send_rows,
        ep,
        split_axis=0,
        concat_axis=0,
        axis_index_groups=turned_order(sources, DISPATCH_FIRST),
        tiled=True,
    )
    marked = 2 * pair_rows
    part = pl.pallas_call(
        hidden_kernel,
        out_shape=jax.ShapeDtypeStruct((rows_total, saved_gu.shape[3]), jnp.bfloat16),
        compiler_params=pltpu.CompilerParams(vmem_limit_bytes=8 << 20),
        name="hidden",
    )(saved_gu[0])
    swap = [(0, 1), (1, 0)]
    marks = pl.pallas_call(
        functools.partial(mark_kernel, first=marked),
        in_specs=[pl.BlockSpec(memory_space=pltpu.VMEM)] * 3,
        out_shape=jax.ShapeDtypeStruct((places, slot_count), jnp.float32),
        scratch_shapes=[pltpu.VMEM((slot_count, slot_count), jnp.float32)],
        compiler_params=pltpu.CompilerParams(vmem_limit_bytes=4 << 20),
        name="marks",
    )(replica_pick, lax.ppermute(replica_pick, "half", swap), slot_expert[None])
    hidden = lax.all_gather(part, "rep", axis=1, tiled=True)
    outputs = pl.pallas_call(
        forward_kernel,
        out_shape=pltpu.VMEM((rows_total, features), jnp.float32),
        compiler_params=pltpu.CompilerParams(vmem_limit_bytes=12 << 20),
        name="forward",
    )(hidden, down_weight[0])
    sent = pl.pallas_call(
        pass_kernel,
        in_specs=[pl.BlockSpec(memory_space=pltpu.VMEM), pl.BlockSpec(memory_space=pl.ANY)],
        out_shape=jax.ShapeDtypeStruct(hidden.shape, hidden.dtype),
        compiler_params=pltpu.CompilerParams(vmem_limit_bytes=4 << 20),
        name="pass",
    )(hidden, marks)
    twin_hidden = lax.ppermute(sent, "half", swap)
    dots = pl.pallas_call(
        dots_kernel,
        in_specs=[pl.BlockSpec(memory_space=pltpu.VMEM)] * 3,
        out_shape=jax.ShapeDtypeStruct((places, 128), jnp.float32),
        scratch_shapes=[pltpu.VMEM((rows_total, 128), jnp.float32)],
        compiler_params=pltpu.CompilerParams(vmem_limit_bytes=8 << 20),
        name="dots",
    )(arrived, outputs, marks)
    met = lax.all_to_all(
        dots.reshape(places, 1, 128),
        "place",
        split_axis=0,
        concat_axis=0,
        axis_index_groups=turned_order(places, PLACE_FIRST),
        tiled=True,
    ).reshape(places, 128)
    group = 2 * copies
    turned = pl.pallas_call(
        functools.partial(turn_kernel, pair_rows=pair_rows, copies=copies),
        out_shape=jax.ShapeDtypeStruct((group, 128), jnp.float32),
        scratch_shapes=[pltpu.VMEM((128, 128), jnp.float32)],
        compiler_params=pltpu.CompilerParams(vmem_limit_bytes=4 << 20),
        name="turn",
    )(met)
    returned = lax.all_to_all(
        turned.reshape(group, 1, 128),
        ("half", "rep"),
        split_axis=0,
        concat_axis=0,
        axis_index_groups=turned_order(group, LINE_FIRST),
        tiled=True,
    )
    steps = 2
    block = hidden_units // steps
    down_grad, order = pl.pallas_call(
        functools.partial(grad_kernel, first=marked),
        grid=(steps,),
        in_specs=[
            pl.BlockSpec(memory_space=pl.ANY),
        ]
        + [pl.BlockSpec(memory_space=pltpu.VMEM)] * 4,
        out_specs=(
            pl.BlockSpec((block, features), lambda i: (i, 0)),
            pl.BlockSpec((8, 128), lambda i: (0, 0)),
        ),
        out_shape=(
            jax.ShapeDtypeStruct((hidden_units, features), jnp.bfloat16),
            jax.ShapeDtypeStruct((8, 128), jnp.float32),
        ),
        scratch_shapes=[
            pltpu.VMEM((rows_total, features), jnp.bfloat16),
            pltpu.VMEM((rows_total, 128), jnp.float32),
        ],
        compiler_params=pltpu.CompilerParams(vmem_limit_bytes=24 << 20),
        name="down_grad",
    )(turned, arrived, met, hidden, twin_hidden)
    route_grad = pl.pallas_call(
        functools.partial(pick_kernel, places=places, copies=copies),
        in_specs=[pl.BlockSpec(memory_space=pltpu.VMEM)] * 3 + [pl.BlockSpec(memory_space=pl.ANY)],
        out_shape=jax.ShapeDtypeStruct((top_count, token_count), jnp.float32),
        scratch_shapes=[pltpu.VMEM((128, 128), jnp.float32)],
        compiler_params=pltpu.CompilerParams(vmem_limit_bytes=4 << 20),
        name="pick",
    )(returned.reshape(group, 128), target, weight_t, order)
    return (down_grad[None], route_grad.T)


def solution(mesh):
    ep, rep = mesh.shape["ep"], mesh.shape["rep"]
    halves = Mesh(mesh.devices.reshape(2, ep // 2, rep), ("half", "place", "rep"))
    ep = ("half", "place")
    placed = (
        P(ep, "rep"),
        P(ep, None),
        P(ep, None),
        P(),
        P(ep, None),
        P(ep, None, None, "rep"),
        P(ep, None, "rep"),
    )
    return jax.shard_map(
        on_device,
        mesh=halves,
        in_specs=placed,
        out_specs=(P(ep, None, "rep"), P(ep, None)),
        check_vma=False,
    )
```

```python
import functools

import jax
import jax.numpy as jnp
from jax import lax
from jax.experimental import pallas as pl
from jax.experimental.pallas import tpu as pltpu
from jax.sharding import Mesh, PartitionSpec as P


DISPATCH_FIRST = 106
PLACE_FIRST = 34
LINE_FIRST = 6


def turned_order(count, first):
    return [[m ^ first for m in range(count)]]


def sources_of(ref):
    step = DISPATCH_FIRST & -DISPATCH_FIRST
    return jnp.concatenate(
        [ref[k ^ DISPATCH_FIRST : (k ^ DISPATCH_FIRST) + step] for k in range(0, ref.shape[0], step)],
        axis=0,
    )


def swap_places(rows):
    count = rows.shape[0]
    row = lax.broadcasted_iota(jnp.int32, rows.shape, 0)
    for bit in (b for b in (1, 2, 4, 8, 16, 32) if b & PLACE_FIRST):
        rows = jnp.where(row & bit == 0, pltpu.roll(rows, count - bit, 0), pltpu.roll(rows, bit, 0))
    return rows


def pack_kernel(ids_ref, weight_ref, slot_expert_ref, pick_ref, grad_ref, out_ref, target_ref, rows_ref, sent):
    top, tokens = ids_ref.shape
    experts = pick_ref.shape[1]
    slots, pair_rows, _ = rows_ref.shape
    slot_expert = slot_expert_ref[...]
    lane = lax.broadcasted_iota(jnp.int32, (1, slots), 1)
    twin = pltpu.roll(slot_expert, slots // 2, 1)
    shared = jnp.where(twin == slot_expert, 1, 0)
    rank = jnp.where((lane >= slots // 2) & (shared > 0), 1.0, 0.0)
    holds = lax.broadcasted_iota(jnp.int32, (experts, slots), 0) == slot_expert
    pick = jnp.dot(
        pick_ref[...].astype(jnp.bfloat16),
        jnp.where(holds, 1.0, 0.0).astype(jnp.bfloat16),
        preferred_element_type=jnp.float32,
    )
    picked = pick == rank
    serves = holds & picked
    slot_of = jnp.sum(jnp.where(serves, lane, 0).astype(jnp.float32), axis=1, keepdims=True)
    other = jnp.where(shared > 0, jnp.where(lane < slots // 2, slots // 2, -(slots // 2)), 0)
    twin_of = slot_of + jnp.sum(
        jnp.where(serves, other, 0).astype(jnp.float32), axis=1, keepdims=True
    )
    expert = lax.broadcasted_iota(jnp.int32, (experts, tokens), 0)
    chosen = [expert == ids_ref[k : k + 1, :] for k in range(top)]
    named = sum(jnp.where(c, 1.0, 0.0) for c in chosen)
    earlier = lax.broadcasted_iota(jnp.int32, (tokens, tokens), 0) < lax.broadcasted_iota(
        jnp.int32, (tokens, tokens), 1
    )
    before = jnp.dot(
        named.astype(jnp.bfloat16),
        jnp.where(earlier, 1.0, 0.0).astype(jnp.bfloat16),
        preferred_element_type=jnp.float32,
    )
    place = slot_of * pair_rows + before
    twin_place = twin_of * pair_rows + before
    row = lax.broadcasted_iota(jnp.int32, (slots * pair_rows, tokens), 0)
    row = row ^ (DISPATCH_FIRST * pair_rows)
    mix = jnp.zeros((slots * pair_rows, tokens), jnp.float32)
    for k in range(top):
        target = jnp.sum(jnp.where(chosen[k], place, 0.0), axis=0, keepdims=True).astype(jnp.int32)
        twin_target = jnp.sum(jnp.where(chosen[k], twin_place, 0.0), axis=0, keepdims=True)
        target_ref[k : k + 1, :] = target
        here = (row == target) | (row == twin_target.astype(jnp.int32))
        mix += jnp.where(here, weight_ref[k : k + 1, :], 0.0)
    mix = mix.astype(jnp.bfloat16)
    count = slots // 2
    copies = []
    for part in range(2):
        here = mix[part * count * pair_rows : (part + 1) * count * pair_rows, :]
        rows = jnp.dot(here, grad_ref[...], preferred_element_type=jnp.float32)
        half = pl.ds(part * count, count)
        rows_ref[half] = rows.astype(rows_ref.dtype).reshape(count, pair_rows, rows.shape[1])
        copy = pltpu.make_async_copy(rows_ref.at[half], out_ref.at[half], sent.at[part])
        copy.start()
        copies.append(copy)
    for copy in copies:
        copy.wait()


def hidden_kernel(saved_ref, out_ref):
    gate = saved_ref[:, 0, :].astype(jnp.float32)
    up = saved_ref[:, 1, :].astype(jnp.float32)
    out_ref[...] = (gate / (1.0 + jnp.exp(-gate)) * up).astype(out_ref.dtype)


def mark_kernel(pick_ref, twin_ref, slot_expert_ref, out_ref, scratch, *, first):
    experts = pick_ref.shape[1]
    slots = slot_expert_ref.shape[1]
    slot_expert = slot_expert_ref[...]
    lane = lax.broadcasted_iota(jnp.int32, (1, slots), 1)
    twin = pltpu.roll(slot_expert, slots // 2, 1)
    rank = jnp.where((lane >= slots // 2) & (twin == slot_expert), 1.0, 0.0)
    holds = lax.broadcasted_iota(jnp.int32, (experts, slots), 0) == slot_expert
    holds = jnp.where(holds, 1.0, 0.0).astype(jnp.bfloat16)
    half = lax.axis_index("half")
    own, other = (
        jnp.dot(ref[...].astype(jnp.bfloat16), holds, preferred_element_type=jnp.float32)
        for ref in (pick_ref, twin_ref)
    )
    scratch[...] = jnp.zeros_like(scratch)
    for source in range(2):
        pick = jnp.where(half == source, own, other)
        scratch[source : source + 1, :] = jnp.where(pick == rank, 1.0, 0.0)
    scratch[...] = scratch[...].T
    places = out_ref.shape[0]
    held = scratch[pl.ds(pl.multiple_of(half * places, places), places), :]
    out_ref[...] = pltpu.roll(held, first, 1)


def pass_kernel(hidden_ref, _, out_ref):
    out_ref[...] = hidden_ref[...]


def forward_kernel(hidden_ref, weight_ref, out_ref):
    out_ref[...] = jnp.dot(hidden_ref[...], weight_ref[...], preferred_element_type=jnp.float32)


def dots_kernel(arrived_ref, outputs_ref, marks_ref, dots_ref, scratch):
    places = dots_ref.shape[0]
    pair_rows = arrived_ref.shape[1]
    rows = sources_of(arrived_ref).reshape(outputs_ref.shape)
    total = jnp.sum(rows.astype(jnp.float32) * outputs_ref[...], axis=1, keepdims=True)
    scratch[...] = jnp.broadcast_to(total, scratch.shape)
    lane = lax.broadcasted_iota(jnp.int32, dots_ref.shape, 1)
    found = marks_ref[...]
    for half in range(2):
        for p in range(pair_rows):
            part = scratch[pl.ds(half * places * pair_rows + p, places, stride=pair_rows), :]
            found = jnp.where(lane == half * pair_rows + p, part, found)
    dots_ref[...] = swap_places(found)


def turn_kernel(arrived_ref, out_ref, *, pair_rows, copies):
    turned = arrived_ref[...].T
    for half in range(2):
        row = jnp.concatenate(
            [turned[half * pair_rows + p : half * pair_rows + p + 1, :] for p in range(pair_rows)], axis=1
        )
        start = half * copies ^ LINE_FIRST // copies * copies
        out_ref[start : start + copies, :] = jnp.broadcast_to(row, (copies, out_ref.shape[1]))


def pick_kernel(returned_ref, target_ref, weight_ref, _, out_ref, scratch, *, places, copies):
    top, tokens = target_ref.shape
    pair_rows = 2
    scratch[...] = jnp.zeros_like(scratch)
    for half in range(2):
        start = half * copies ^ LINE_FIRST // copies * copies
        scratch[half : half + 1, :] = jnp.sum(
            returned_ref[start : start + copies, :], axis=0, keepdims=True
        )
    returned = scratch[...].T
    row = lax.broadcasted_iota(jnp.int32, (returned.shape[0], tokens), 0)
    for k in range(top):
        target = target_ref[k : k + 1, :]
        slot = target // pair_rows
        here = row == (target % pair_rows) * places + (slot % places ^ PLACE_FIRST)
        found = jnp.where(here, jnp.where(slot < places, returned[:, :1], returned[:, 1:2]), 0.0)
        weight = weight_ref[k : k + 1, :].astype(jnp.bfloat16).astype(jnp.float32)
        out_ref[k : k + 1, :] = jnp.sum(found, axis=0, keepdims=True) / weight


def grad_kernel(
    _, arrived_ref, marks_ref, hidden_ref, twin_hidden_ref, out_ref, order_ref, rows_ref, own_ref, *, first
):
    places = marks_ref.shape[0]
    pair_rows = arrived_ref.shape[1]

    @pl.when(pl.program_id(0) == 0)
    def _():
        rows_ref[...] = sources_of(arrived_ref).reshape(rows_ref.shape)
        marks = swap_places(marks_ref[...])
        for half in range(2):
            mark = jnp.broadcast_to(marks[:, first + half : first + half + 1], marks.shape)
            for p in range(pair_rows):
                own_ref[pl.ds(half * places * pair_rows + p, places, stride=pair_rows), :] = mark
        order_ref[...] = jnp.zeros_like(order_ref)

    own = own_ref[:, :1] > 0.5
    block = out_ref.shape[0]
    here = pl.ds(pl.multiple_of(pl.program_id(0) * block, block), block)
    hidden = jnp.where(own, hidden_ref[:, here], twin_hidden_ref[:, here])
    out_ref[...] = lax.dot_general(
        hidden, rows_ref[...], (((0,), (0,)), ((), ())), preferred_element_type=jnp.float32
    ).astype(out_ref.dtype)


def on_device(out_grad, route_weight, expert_ids, slot_expert, replica_pick, saved_gu, down_weight):
    ep = ("half", "place")
    sources = lax.axis_size(ep)
    places, copies = lax.axis_size("place"), lax.axis_size("rep")
    token_count, top_count = expert_ids.shape
    slot_count = slot_expert.shape[0]
    rows_total = saved_gu.shape[1]
    pair_rows = rows_total // sources
    features = out_grad.shape[1]
    hidden_units = down_weight.shape[1]
    ids_t = expert_ids.T
    weight_t = route_weight.T
    send_rows, target = pl.pallas_call(
        pack_kernel,
        out_shape=(
            jax.ShapeDtypeStruct((slot_count, pair_rows, features), jnp.bfloat16),
            jax.ShapeDtypeStruct((top_count, token_count), jnp.int32),
        ),
        out_specs=(pl.BlockSpec(memory_space=pl.ANY), pl.BlockSpec(memory_space=pltpu.VMEM)),
        scratch_shapes=[
            pltpu.VMEM((slot_count, pair_rows, features), jnp.bfloat16),
            pltpu.SemaphoreType.DMA((2,)),
        ],
        name="pack",
    )(ids_t, weight_t, slot_expert[None], replica_pick, out_grad)
    arrived = lax.all_to_all(
        send_rows,
        ep,
        split_axis=0,
        concat_axis=0,
        axis_index_groups=turned_order(sources, DISPATCH_FIRST),
        tiled=True,
    )
    marked = 2 * pair_rows
    part = pl.pallas_call(
        hidden_kernel,
        out_shape=jax.ShapeDtypeStruct((rows_total, saved_gu.shape[3]), jnp.bfloat16),
        compiler_params=pltpu.CompilerParams(vmem_limit_bytes=8 << 20),
        name="hidden",
    )(saved_gu[0])
    swap = [(0, 1), (1, 0)]
    marks = pl.pallas_call(
        functools.partial(mark_kernel, first=marked),
        in_specs=[pl.BlockSpec(memory_space=pltpu.VMEM)] * 3,
        out_shape=jax.ShapeDtypeStruct((places, slot_count), jnp.float32),
        scratch_shapes=[pltpu.VMEM((slot_count, slot_count), jnp.float32)],
        compiler_params=pltpu.CompilerParams(vmem_limit_bytes=4 << 20),
        name="marks",
    )(replica_pick, lax.ppermute(replica_pick, "half", swap), slot_expert[None])
    hidden = lax.all_gather(part, "rep", axis=1, tiled=True)
    outputs = pl.pallas_call(
        forward_kernel,
        out_shape=pltpu.VMEM((rows_total, features), jnp.float32),
        compiler_params=pltpu.CompilerParams(vmem_limit_bytes=12 << 20),
        name="forward",
    )(hidden, down_weight[0])
    sent = pl.pallas_call(
        pass_kernel,
        in_specs=[pl.BlockSpec(memory_space=pltpu.VMEM), pl.BlockSpec(memory_space=pl.ANY)],
        out_shape=jax.ShapeDtypeStruct(hidden.shape, hidden.dtype),
        compiler_params=pltpu.CompilerParams(vmem_limit_bytes=4 << 20),
        name="pass",
    )(hidden, marks)
    twin_hidden = lax.ppermute(sent, "half", swap)
    dots = pl.pallas_call(
        dots_kernel,
        in_specs=[pl.BlockSpec(memory_space=pltpu.VMEM)] * 3,
        out_shape=jax.ShapeDtypeStruct((places, 128), jnp.float32),
        scratch_shapes=[pltpu.VMEM((rows_total, 128), jnp.float32)],
        compiler_params=pltpu.CompilerParams(vmem_limit_bytes=8 << 20),
        name="dots",
    )(arrived, outputs, marks)
    met = lax.all_to_all(
        dots.reshape(places, 1, 128),
        "place",
        split_axis=0,
        concat_axis=0,
        axis_index_groups=turned_order(places, PLACE_FIRST),
        tiled=True,
    ).reshape(places, 128)
    group = 2 * copies
    turned = pl.pallas_call(
        functools.partial(turn_kernel, pair_rows=pair_rows, copies=copies),
        out_shape=jax.ShapeDtypeStruct((group, 128), jnp.float32),
        compiler_params=pltpu.CompilerParams(vmem_limit_bytes=4 << 20),
        name="turn",
    )(met)
    returned = lax.all_to_all(
        turned.reshape(group, 1, 128),
        ("half", "rep"),
        split_axis=0,
        concat_axis=0,
        axis_index_groups=turned_order(group, LINE_FIRST),
        tiled=True,
    )
    steps = 2
    block = hidden_units // steps
    down_grad, order = pl.pallas_call(
        functools.partial(grad_kernel, first=marked),
        grid=(steps,),
        in_specs=[
            pl.BlockSpec(memory_space=pl.ANY),
        ]
        + [pl.BlockSpec(memory_space=pltpu.VMEM)] * 4,
        out_specs=(
            pl.BlockSpec((block, features), lambda i: (i, 0)),
            pl.BlockSpec((8, 128), lambda i: (0, 0)),
        ),
        out_shape=(
            jax.ShapeDtypeStruct((hidden_units, features), jnp.bfloat16),
            jax.ShapeDtypeStruct((8, 128), jnp.float32),
        ),
        scratch_shapes=[
            pltpu.VMEM((rows_total, features), jnp.bfloat16),
            pltpu.VMEM((rows_total, 128), jnp.float32),
        ],
        compiler_params=pltpu.CompilerParams(vmem_limit_bytes=24 << 20),
        name="down_grad",
    )(turned, arrived, met, hidden, twin_hidden)
    route_grad = pl.pallas_call(
        functools.partial(pick_kernel, places=places, copies=copies),
        in_specs=[pl.BlockSpec(memory_space=pltpu.VMEM)] * 3 + [pl.BlockSpec(memory_space=pl.ANY)],
        out_shape=jax.ShapeDtypeStruct((top_count, token_count), jnp.float32),
        scratch_shapes=[pltpu.VMEM((8, 128), jnp.float32)],
        compiler_params=pltpu.CompilerParams(vmem_limit_bytes=4 << 20),
        name="pick",
    )(returned.reshape(group, 128), target, weight_t, order)
    return (down_grad[None], route_grad.T)


def solution(mesh):
    ep, rep = mesh.shape["ep"], mesh.shape["rep"]
    halves = Mesh(mesh.devices.reshape(2, ep // 2, rep), ("half", "place", "rep"))
    ep = ("half", "place")
    placed = (
        P(ep, "rep"),
        P(ep, None),
        P(ep, None),
        P(),
        P(ep, None),
        P(ep, None, None, "rep"),
        P(ep, None, "rep"),
    )
    return jax.shard_map(
        on_device,
        mesh=halves,
        in_specs=placed,
        out_specs=(P(ep, None, "rep"), P(ep, None)),
        check_vma=False,
    )
```
